32 devices in a mesh: grp: 2 (over y), row: 4 (over z), col: 4 (over x, core).
Axes of the slice: x: 2, y: 2, z: 4, core: 2. Of those that a mesh axis runs over, the one named last changes fastest.
Arguments:
- front: float32 [2048, 2048], P('col', ('grp', 'row')), may hold values from -9 to 11, as said below
- child_blocks: float32 [2, 2048, 2048], P('grp', ('row', 'col')), may hold values from -4.5 to 4.5, as said below
- child_map: int32 [2, 16], replicated, may hold values from 0 to 15, as said below
Outputs:
- factor: float32 [2048, 2048], P('col', ('grp', 'row'))
The draws below stay inside these ranges and needn't reach their ends.
Inputs may be any that keep to these rules, and one draw needn't show every extreme that they name: `front`: symmetric positive definite. `child_blocks`: each child's block is symmetric positive semidefinite. `child_map`: the blocks of one child are distinct; block q of a child, with q modulo the size of the col axis equal to k, lies in parent blocks k * 2 * 2 to (k + 1) * 2 * 2 - 1; at most 2 blocks of one child fall in one aligned group of 2 parent blocks, and in every draw some group holds 2.
All inputs are finite; a program needn't handle non-finite values.
Results may differ from the reference program's by a relative error of at most 0.00005.
Values sent between devices are 32-bit elements; how exact they have to be, the bound alone decides.
No kernel may reach another device: no remote copies, remote signals or barrier semaphores. Data moves between devices by JAX's collectives and lax.ppermute only.
A program may use at most 128 MiB of HBM per device.

```python
import jax
import jax.numpy as jnp
from jax import lax

BLK = 128
BPO = 2
M = 2048
PIVOTS = 256
CM = 2048
OPC = 2
CAP = 2
N_GRP = 2
N_ROW = 4
N_COL = 4


def symmetric_part(matrix):
    return (matrix + jnp.swapaxes(matrix, -1, -2)) * 0.5


def one_permutation(subkey):
    return jax.random.permutation(subkey, OPC * CAP)


def draw_front(key, part):
    key = jax.random.fold_in(key, 11)
    key_basis, key_shift = jax.random.split(key, 2)
    basis = jnp.clip(jax.random.normal(key_basis, (M, PIVOTS), jnp.float32), -3.0, 3.0)
    shift = jax.random.uniform(key_shift, (M,), jnp.float32, 1.0, 2.0)
    coupled = symmetric_part(jnp.dot(basis, basis.T, precision=lax.Precision.HIGHEST) / PIVOTS)
    positions = jnp.arange(M)
    on_diagonal = positions[:, None] == positions[None, :]
    return (coupled + jnp.where(on_diagonal, shift[None, :], 0.0)).astype(jnp.float32)


def draw_child_blocks(key, part):
    key = jax.random.fold_in(key, 12)
    basis = jnp.clip(jax.random.normal(key, (N_GRP, CM, 256), jnp.float32), -3.0, 3.0)
    gram = jnp.einsum('gik,gjk->gij', basis, basis, precision=lax.Precision.HIGHEST) * (0.5 / 256)
    return symmetric_part(gram).astype(jnp.float32)


def draw_child_map(key, part):
    key = jax.random.fold_in(key, 13)
    key_perm, key_within = jax.random.split(key)
    perms = jax.vmap(one_permutation)(jax.random.split(key_perm, N_GRP * N_COL))[:, :N_ROW]
    col_of = (jnp.arange(N_GRP * N_COL) % N_COL)[:, None]
    owner_ids = perms // CAP + col_of * OPC
    within = perms % CAP * (BPO // CAP) + jax.random.randint(key_within, perms.shape, 0, BPO // CAP)
    blocks = owner_ids * BPO + within
    return blocks.reshape(N_GRP, N_COL, N_ROW).transpose(0, 2, 1).reshape(N_GRP, N_ROW * N_COL).astype(jnp.int32)


def setup_inputs(seed: int = 0) -> dict:
    keys = jax.random.split(jax.random.key(seed), 4)
    front = draw_front(jax.random.fold_in(keys[3], 71), 0)
    child_blocks = draw_child_blocks(jax.random.fold_in(keys[3], 71), 0)
    child_map = draw_child_map(jax.random.fold_in(keys[3], 71), 0)
    return dict(front=front, child_blocks=child_blocks, child_map=child_map)


def reference(front, child_blocks, child_map):
    assembled = front
    offsets = jnp.arange(BLK, dtype=jnp.int32)
    for child_id in range(N_GRP):
        row_index = (child_map[child_id][:, None] * BLK + offsets[None, :]).reshape(-1).astype(jnp.int32)
        assembled = assembled.at[row_index[:, None], row_index[None, :]].add(child_blocks[child_id])
    pivot_block = assembled[:PIVOTS, :PIVOTS]
    lower_block = jnp.linalg.cholesky(pivot_block)
    coupling = lax.linalg.triangular_solve(lower_block, assembled[PIVOTS:, :PIVOTS], left_side=False, lower=True, transpose_a=True)
    schur = assembled[PIVOTS:, PIVOTS:] - jnp.dot(coupling, coupling.T, precision=lax.Precision.HIGHEST)
    top_rows = jnp.concatenate([lower_block, jnp.zeros((PIVOTS, M - PIVOTS), assembled.dtype)], axis=1)
    bottom_rows = jnp.concatenate([coupling, schur], axis=1)
    return jnp.concatenate([top_rows, bottom_rows], axis=0)
```

```python
import functools

import jax
import jax.numpy as jnp
from jax import lax
from jax.experimental import pallas as pl
from jax.experimental.pallas import tpu as pltpu
from jax.sharding import PartitionSpec as P

BLK = 128
PIVOTS = 256
OWNER = ("grp", "row")
HIGHEST = lax.Precision.HIGHEST
VMEM = pl.BlockSpec(memory_space=pltpu.VMEM)
SMEM = pl.BlockSpec(memory_space=pltpu.SMEM)
ANY = pl.BlockSpec(memory_space=pl.ANY)
PARAMS = pltpu.CompilerParams(vmem_limit_bytes=48 * 1024 * 1024)


def f32(*shape):
    return jax.ShapeDtypeStruct(shape, jnp.float32)


def owner_of():
    return lax.axis_index("grp") * lax.axis_size("row") + lax.axis_index("row")


def invert_map(map_ref, inv_ref, grp):
    blocks = inv_ref.shape[0]
    for q in range(blocks):
        inv_ref[map_ref[grp, q]] = q


def split_panel_kernel(map_ref, strip_ref, *refs):
    outs, (inv_ref, sems) = refs[:-2], refs[-2:]
    pieces = len(outs)
    rows, width = outs[0].shape
    grp = lax.axis_index("grp")
    me = owner_of()
    invert_map(map_ref, inv_ref, grp)
    copies = []
    for d in range(pieces):
        for s in range(width // BLK):
            source = inv_ref[s]
            copies.append(
                pltpu.make_async_copy(
                    strip_ref.at[pl.ds((me ^ d) * rows, rows), pl.ds(source * BLK, BLK)],
                    outs[d].at[:, pl.ds(s * BLK, BLK)],
                    sems.at[d, s],
                )
            )
    for copy in copies:
        copy.start()
    for copy in copies:
        copy.wait()


def split_strip_kernel(map_ref, strip_ref, *refs):
    outs, (inv_ref, sems) = refs[:-2], refs[-2:]
    pieces = len(outs)
    _, width = outs[0].shape
    per = width // BLK
    grp = lax.axis_index("grp")
    me = owner_of()
    invert_map(map_ref, inv_ref, grp)
    copies = []
    for d in range(pieces):
        for s in range(per):
            source = inv_ref[(me ^ d) * per + s]
            copies.append(
                pltpu.make_async_copy(
                    strip_ref.at[:, pl.ds(source * BLK, BLK)],
                    outs[d].at[:, pl.ds(s * BLK, BLK)],
                    sems.at[d, s],
                )
            )
    for copy in copies:
        copy.start()
    for copy in copies:
        copy.wait()


def local_block(map_ref, source, row_blocks):
    n_row, n_col = lax.axis_size("row"), lax.axis_size("col")
    col = lax.axis_index("col")
    grp, row = source // n_row, source % n_row
    return map_ref[grp, row * n_col + col] - col * row_blocks


def sum_panel_kernel(map_ref, *refs):
    out_ref = refs[-1]
    pieces = (len(refs) - 1) // 2
    fronts, strips = refs[:pieces], refs[pieces:-1]
    me = owner_of()
    total = jnp.where(me == 0, fronts[0][...], 0.0)
    for ref in fronts[1:]:
        total = total + ref[...]
    out_ref[...] = total
    for d in range(pieces):
        block = local_block(map_ref, me ^ d, out_ref.shape[0])
        out_ref[block] = out_ref[block] + strips[d][...]


def finish_kernel(map_ref, front_ref, rows_c_ref, rows_o_ref, inv_ref, lower_ref, *refs):
    strips, out_ref = refs[:-1], refs[-1]
    rows, width = out_ref.shape
    col = lax.axis_index("col")
    me = owner_of()
    row_blocks = rows // BLK
    inv = inv_ref[...]
    dims = (((1,), (1,)), ((), ()))
    dot = functools.partial(
        lax.dot_general, dimension_numbers=dims, precision=HIGHEST, preferred_element_type=jnp.float32
    )
    left = dot(rows_c_ref[...], inv)

    @pl.when(me == 0)
    def _():
        out_ref[...] = left

        @pl.when(col == 0)
        def _():
            out_ref[:PIVOTS, :] = lower_ref[...]

    @pl.when(me != 0)
    def _():
        right = dot(rows_o_ref[...], inv)
        out_ref[...] = front_ref[...] - dot(left, right)
        for d, ref in enumerate(strips):
            start = pl.multiple_of(local_block(map_ref, me ^ d, row_blocks) * BLK, BLK)
            out_ref[pl.ds(start, BLK), :] += ref[...]

        @pl.when(col == 0)
        def _():
            out_ref[:PIVOTS, :] = jnp.zeros((PIVOTS, width), jnp.float32)


def exchange(value, d, skip_root=False):
    owners = lax.axis_size(OWNER)
    perm = [(i, i ^ d) for i in range(owners) if not (skip_root and i == d)]
    return lax.ppermute(value, OWNER, perm)


def from_root(value, axis, root):
    mine = lax.axis_index(axis) == root
    return lax.psum(jnp.where(mine, value, jnp.zeros_like(value)), axis)


def gather_wide(front, strip, child_map):
    n_row, n_col = lax.axis_size("row"), lax.axis_size("col")
    owners = lax.axis_size(OWNER)
    rows, width = front.shape
    row_blocks = rows // BLK
    blocks = owners * width // BLK
    me = owner_of()
    col = lax.axis_index("col")
    hits = child_map[lax.axis_index("grp")][None, :] == jnp.arange(blocks)[:, None]
    source = jnp.argmax(hits, axis=1)
    taken = jnp.take(strip.reshape(BLK, -1, BLK), source, axis=1)
    taken = jnp.where(jnp.any(hits, axis=1)[None, :, None], taken, 0.0)
    outgoing = taken.reshape(BLK, owners, width).transpose(1, 0, 2)
    incoming = lax.all_to_all(outgoing, OWNER, split_axis=0, concat_axis=0, tiled=True)
    ids = jnp.arange(owners)
    places = child_map[ids // n_row, ids % n_row * n_col + col] - col * row_blocks
    assembled = front.reshape(row_blocks, BLK, width).at[places].add(incoming).reshape(rows, width)
    rows_c = from_root(assembled, OWNER, 0)
    pivot = from_root(rows_c[:PIVOTS], "col", 0)
    part = lax.dynamic_slice_in_dim(rows_c, me * width % rows, width, 0)
    rows_o = jnp.zeros((width, width), jnp.float32)
    for c in range(n_col):
        low = c * rows // width
        sent = from_root(part, "col", c)
        rows_o = jnp.where((me >= low) & (me < low + rows // width), sent, rows_o)
    return assembled, rows_c, rows_o, pivot, []


def gather_pieces(front, strip, child_map):
    n_col = lax.axis_size("col")
    owners = lax.axis_size(OWNER)
    rows, width = front.shape
    row_blocks = rows // BLK
    part = BLK // owners
    blocks = owners * width // BLK
    me = owner_of()
    col = lax.axis_index("col")

    split = functools.partial(
        pl.pallas_call,
        in_specs=[SMEM, ANY],
        out_specs=[ANY] * owners,
        scratch_shapes=[pltpu.SMEM((blocks,), jnp.int32), pltpu.SemaphoreType.DMA((owners, width // BLK))],
    )
    panel_pieces = split(split_panel_kernel, out_shape=[f32(part, width)] * owners, name="split_panel")(child_map, strip)
    strip_pieces = split(split_strip_kernel, out_shape=[f32(BLK, width)] * owners, name="split_strip")(child_map, strip)

    front_parts = front.reshape(row_blocks, owners, part, width)
    fronts = [front_parts[:, 0]] + [
        lax.ppermute(front_parts[:, k], OWNER, [(0, k)]) for k in range(1, owners)
    ]
    strips = [panel_pieces[0]] + [exchange(panel_pieces[d], d) for d in range(1, owners)]
    mine = pl.pallas_call(
        sum_panel_kernel,
        out_shape=f32(row_blocks, part, width),
        in_specs=[SMEM] + [VMEM] * (2 * owners),
        out_specs=VMEM,
        compiler_params=PARAMS,
        name="sum_panel",
    )(child_map, *fronts, *strips)

    top = mine[: PIVOTS // BLK]
    tops = jnp.where(col == 0, top, 0.0)
    for c in range(1, n_col):
        tops = tops + lax.ppermute(top, "col", [(0, c)])
    gathered = [tops] + [exchange(tops, d) for d in range(1, owners)]
    order = jnp.arange(owners) ^ me
    pivot = jnp.stack(gathered)[order]
    pivot = pivot.transpose(1, 0, 2, 3).reshape(PIVOTS, width)

    arrived = [strip_pieces[0]] + [exchange(strip_pieces[d], d, True) for d in range(1, owners)]

    rows_c = lax.all_gather(mine, OWNER).transpose(1, 0, 2, 3).reshape(rows, width)
    root = me * width // rows
    own_part = lax.dynamic_slice_in_dim(rows_c, me * width % rows, width, 0)
    rows_o = jnp.where(col == root, own_part, 0.0)
    for e in range(1, n_col):
        perm = []
        for o in range(owners):
            c = o * width // rows
            perm.append((o * n_col + c, o * n_col + (c ^ e)))
        rows_o = rows_o + lax.ppermute(own_part, OWNER + ("col",), perm)

    return front, rows_c, rows_o, pivot, arrived


def body(front, child_blocks, child_map):
    owners = lax.axis_size(OWNER)
    rows, width = front.shape
    blocks = owners * width // BLK
    few = BLK % (owners * 8) == 0 and child_map.shape[1] == blocks
    gather = gather_pieces if few else gather_wide
    base, rows_c, rows_o, pivot, arrived = gather(front, child_blocks[0], child_map)
    lower = jnp.linalg.cholesky(pivot)
    inverse = lax.linalg.triangular_solve(
        lower, jnp.eye(PIVOTS, dtype=jnp.float32), left_side=True, lower=True
    )
    return pl.pallas_call(
        finish_kernel,
        out_shape=f32(rows, width),
        in_specs=[SMEM] + [VMEM] * (5 + len(arrived)),
        out_specs=VMEM,
        compiler_params=PARAMS,
        name="finish",
    )(child_map, base, rows_c, rows_o, inverse, lower, *arrived)


def solution(mesh):
    return jax.shard_map(
        body,
        mesh=mesh,
        in_specs=(P("col", ("grp", "row")), P("grp", ("row", "col"), None), P()),
        out_specs=P("col", ("grp", "row")),
        check_vma=False,
    )
```

```python
import jax
import jax.numpy as jnp
from jax import lax
from jax.experimental import pallas as pl
from jax.experimental.pallas import tpu as pltpu
from jax.sharding import PartitionSpec as P

BLK = 128
PIVOTS = 256
OWNER = ("grp", "row")
HIGHEST = lax.Precision.HIGHEST
SUB = 8
VMEM = pl.BlockSpec(memory_space=pltpu.VMEM)
SMEM = pl.BlockSpec(memory_space=pltpu.SMEM)
PARAMS = pltpu.CompilerParams(vmem_limit_bytes=48 * 1024 * 1024)


def f32(*shape):
    return jax.ShapeDtypeStruct(shape, jnp.float32)


def owner_of():
    return lax.axis_index("grp") * lax.axis_size("row") + lax.axis_index("row")


def dot(a, b, ca, cb):
    return lax.dot_general(
        a, b, (((ca,), (cb,)), ((), ())), precision=HIGHEST, preferred_element_type=jnp.float32
    )


def factor_small(cols):
    n = len(cols)
    d = [[cols[k][i] if i >= k else None for k in range(n)] for i in range(n)]
    low = [[None] * n for _ in range(n)]
    inv = [[None] * n for _ in range(n)]
    for k in range(n):
        root = lax.rsqrt(d[k][k])
        root = root * (1.5 - 0.5 * d[k][k] * root * root)
        inv[k][k] = root
        for i in range(k + 1, n):
            low[i][k] = d[i][k] * root
        for i in range(k + 1, n):
            for j in range(k + 1, i + 1):
                d[i][j] = d[i][j] - low[i][k] * low[j][k]
        for j in range(k):
            total = low[k][j] * inv[j][j]
            for m in range(j + 1, k):
                total = total + low[k][m] * inv[m][j]
            inv[k][j] = -root * total
    return inv


def factor_block(groups):
    count = len(groups)
    shape = (SUB, BLK)
    sub = lax.broadcasted_iota(jnp.int32, shape, 0)
    lane = lax.broadcasted_iota(jnp.int32, shape, 1)
    spread_row = lambda v, i: jnp.broadcast_to(v[i : i + 1, :], shape)
    spread_col = lambda v, c: jnp.broadcast_to(v[:, c : c + 1], shape)
    upper, inverse = [], []
    groups = list(groups)
    for b in range(count):
        base = SUB * b
        cur = groups[b]
        here = [spread_col(cur, base + k) for k in range(SUB)]
        inv = factor_small([[spread_row(here[k], i) for i in range(SUB)] for k in range(SUB)])
        inv_col = []
        for k in range(SUB):
            col = jnp.where(sub == k, inv[k][k], 0.0)
            for i in range(k + 1, SUB):
                col = jnp.where(sub == i, inv[i][k], col)
            inv_col.append(col)
        done = inv_col[0] * spread_row(cur, 0)
        for k in range(1, SUB):
            done = done + inv_col[k] * spread_row(cur, k)
        upper.append(jnp.where(lane >= base + sub, done, 0.0))
        kept = done
        for k in range(SUB):
            kept = jnp.where(lane == base + k, inv_col[k], kept)
        inverse.append(jnp.where(lane <= base + sub, kept, 0.0))
        if b + 1 == count:
            break
        inside = (lane >= base) & (lane < base + SUB)
        nxt = groups[b + 1]
        after = [spread_col(nxt, base + k) for k in range(SUB)]
        nxt = jnp.where(inside, 0.0, nxt)
        for i in range(SUB):
            low = after[0] * inv[i][0]
            for k in range(1, i + 1):
                low = low + after[k] * inv[i][k]
            nxt = nxt - low * spread_row(kept, i)
        groups[b + 1] = nxt
        if b + 2 < count:
            change = dot(done[:, base + 2 * SUB :], kept, 0, 0)
            for j in range(b + 2, count):
                at = SUB * (j - b - 2)
                groups[j] = jnp.where(inside, 0.0, groups[j]) - change[at : at + SUB]
    return upper, inverse


def factor_pivot(pivot_ref, upper_ref, inverse_ref):
    halves = pivot_ref.shape[0] // BLK
    assert halves == 2
    zero = jnp.zeros((BLK, BLK), jnp.float32)

    def run(h, source):
        rows = slice(h * BLK, (h + 1) * BLK)
        upper, inverse = factor_block([source[SUB * g : SUB * (g + 1)] for g in range(BLK // SUB)])
        for g in range(BLK // SUB):
            at = slice(h * BLK + SUB * g, h * BLK + SUB * (g + 1))
            upper_ref[at, rows] = upper[g]
            inverse_ref[at, rows] = inverse[g]

    run(0, pivot_ref[:BLK, :BLK])
    first = inverse_ref[:BLK, :BLK]
    side = dot(first, pivot_ref[:BLK, BLK:], 1, 0)
    upper_ref[:BLK, BLK:] = side
    upper_ref[BLK:, :BLK] = zero
    inverse_ref[:BLK, BLK:] = zero
    run(1, pivot_ref[BLK:, BLK:] - dot(side, side, 0, 0))
    second = inverse_ref[BLK:, BLK:]
    inverse_ref[BLK:, :BLK] = -dot(second, dot(side, first, 0, 0), 1, 0)


def split_kernel(map_ref, strip_ref, front_ref, *refs):
    top_ref, rest_ref, out_ref, inv_ref = refs
    owners, part = top_ref.shape[0], top_ref.shape[2]
    per = out_ref.shape[2] // BLK
    grp, row, col = (lax.axis_index(a) for a in ("grp", "row", "col"))
    n_row, n_col = lax.axis_size("row"), lax.axis_size("col")
    me = grp * n_row + row
    for q in range(map_ref.shape[1]):
        inv_ref[map_ref[grp, q]] = q
    for k in range(owners):
        for s in range(per):
            at = pl.multiple_of(inv_ref[k * per + s] * BLK, BLK)
            out_ref[k, :, s * BLK : (s + 1) * BLK] = strip_ref[:, pl.ds(at, BLK)]
    row_blocks = front_ref.shape[0] // BLK
    tops = top_ref.shape[1]
    mine = map_ref[grp, row * n_col + col] - col * row_blocks
    for k in range(owners):
        piece = out_ref[0, part * k : part * (k + 1), :]
        for b in range(row_blocks):
            at = b * BLK + part * k
            value = jnp.where(mine == b, piece, 0.0)
            value = value + jnp.where(me == 0, front_ref[at : at + part, :], 0.0)
            if b < tops:
                top_ref[k, b] = value
            else:
                rest_ref[k, b - tops] = value


def pivot_kernel(pieces_ref, upper_ref, inverse_ref, pivot_ref):
    owners, blocks, part, _ = pieces_ref.shape
    for b in range(blocks):
        for k in range(owners):
            at = b * BLK + part * k
            pivot_ref[at : at + part, :] = pieces_ref[k, b]
    factor_pivot(pivot_ref, upper_ref, inverse_ref)


def finish_kernel(map_ref, front_ref, rows_c_ref, rows_o_ref, upper_ref, inverse_ref, *refs):
    strips_ref, out_ref = (refs[0] if len(refs) == 2 else None), refs[-1]
    rows, width = out_ref.shape
    n_row, n_col = lax.axis_size("row"), lax.axis_size("col")
    col = lax.axis_index("col")
    me = owner_of()
    row_blocks = rows // BLK
    inv = inverse_ref[...]

    def solved(ref):
        if len(ref.shape) == 2:
            return dot(ref[...], inv, 1, 1)
        owners, blocks = ref.shape[:2]
        whole = jnp.concatenate([ref[k, b] for b in range(blocks) for k in range(owners)], axis=0)
        return dot(whole, inv, 1, 1)

    left = solved(rows_c_ref)

    @pl.when(me == 0)
    def _():
        out_ref[...] = left

        @pl.when(col == 0)
        def _():
            out_ref[:PIVOTS, :] = upper_ref[...].T

    @pl.when(me != 0)
    def _():
        right = solved(rows_o_ref)
        out_ref[...] = front_ref[...] - dot(left, right, 1, 1)
        if strips_ref is not None:
            for i in range(strips_ref.shape[0]):
                local = map_ref[i // n_row, i % n_row * n_col + col] - col * row_blocks
                start = pl.multiple_of(local * BLK, BLK)
                out_ref[pl.ds(start, BLK), :] += strips_ref[i]

        @pl.when(col == 0)
        def _():
            out_ref[:PIVOTS, :] = jnp.zeros((PIVOTS, width), jnp.float32)


def from_root(value, axis, root):
    mine = lax.axis_index(axis) == root
    return lax.psum(jnp.where(mine, value, jnp.zeros_like(value)), axis)


def gather_wide(front, strip, child_map):
    n_row, n_col = lax.axis_size("row"), lax.axis_size("col")
    owners = lax.axis_size(OWNER)
    rows, width = front.shape
    row_blocks = rows // BLK
    blocks = owners * width // BLK
    me = owner_of()
    col = lax.axis_index("col")
    hits = child_map[lax.axis_index("grp")][None, :] == jnp.arange(blocks)[:, None]
    source = jnp.argmax(hits, axis=1)
    taken = jnp.take(strip.reshape(BLK, -1, BLK), source, axis=1)
    taken = jnp.where(jnp.any(hits, axis=1)[None, :, None], taken, 0.0)
    outgoing = taken.reshape(BLK, owners, width).transpose(1, 0, 2)
    incoming = lax.all_to_all(outgoing, OWNER, split_axis=0, concat_axis=0, tiled=True)
    ids = jnp.arange(owners)
    places = child_map[ids // n_row, ids % n_row * n_col + col] - col * row_blocks
    assembled = front.reshape(row_blocks, BLK, width).at[places].add(incoming).reshape(rows, width)
    rows_c = from_root(assembled, OWNER, 0)
    pivot = from_root(rows_c[:PIVOTS], "col", 0)
    part = lax.dynamic_slice_in_dim(rows_c, me * width % rows, width, 0)
    rows_o = jnp.zeros((width, width), jnp.float32)
    for c in range(n_col):
        low = c * rows // width
        sent = from_root(part, "col", c)
        rows_o = jnp.where((me >= low) & (me < low + rows // width), sent, rows_o)
    return assembled, rows_c, rows_o, pivot.reshape(1, PIVOTS // BLK, BLK, width), []


def swap(pieces):
    return lax.all_to_all(pieces, OWNER, split_axis=0, concat_axis=0, tiled=True)


def spread(piece):
    return swap(jnp.broadcast_to(piece[None], (lax.axis_size(OWNER),) + piece.shape))


def gather_pieces(front, strip, child_map):
    n_col = lax.axis_size("col")
    owners = lax.axis_size(OWNER)
    rows, width = front.shape
    row_blocks = rows // BLK
    tops = PIVOTS // BLK
    part = BLK // owners
    me = owner_of()
    col = lax.axis_index("col")
    top, rest, strips = pl.pallas_call(
        split_kernel,
        out_shape=[f32(owners, tops, part, width), f32(owners, row_blocks - tops, part, width), f32(owners, BLK, width)],
        in_specs=[SMEM, VMEM, VMEM],
        out_specs=[VMEM] * 3,
        scratch_shapes=[pltpu.SMEM((child_map.shape[1],), jnp.int32)],
        compiler_params=PARAMS,
        name="split",
    )(child_map, strip, front)

    top = jnp.sum(swap(top), axis=0)
    pivot = jnp.where(col == 0, top, 0.0)
    for c in range(1, n_col):
        pivot = pivot + lax.ppermute(top, "col", [(0, c)])
    pivot = spread(pivot)
    rest = jnp.sum(swap(rest), axis=0)
    rows_c = spread(jnp.concatenate([top, rest], axis=0))
    strips = swap(strips)

    root = me * width // rows
    own_part = lax.dynamic_slice_in_dim(rows_c, me * width % rows // BLK, width // BLK, 1)
    rows_o = jnp.where(col == root, own_part, 0.0)
    for e in range(1, n_col):
        perm = []
        for o in range(owners):
            c = o * width // rows
            perm.append((o * n_col + c, o * n_col + (c ^ e)))
        rows_o = rows_o + lax.ppermute(own_part, OWNER + ("col",), perm)
    return front, rows_c, rows_o, pivot, [strips]


def body(front, child_blocks, child_map):
    owners = lax.axis_size(OWNER)
    rows, width = front.shape
    blocks = owners * width // BLK
    few = BLK % (owners * 8) == 0 and child_map.shape[1] == blocks
    gather = gather_pieces if few else gather_wide
    base, rows_c, rows_o, pivot, strips = gather(front, child_blocks[0], child_map)
    upper, inverse = pl.pallas_call(
        pivot_kernel,
        out_shape=[f32(PIVOTS, PIVOTS)] * 2,
        in_specs=[VMEM],
        out_specs=[VMEM] * 2,
        scratch_shapes=[pltpu.VMEM((PIVOTS, PIVOTS), jnp.float32)],
        compiler_params=PARAMS,
        cost_estimate=pl.CostEstimate(flops=20_000_000_000, bytes_accessed=1 << 20, transcendentals=0),
        name="pivot",
    )(pivot)
    return pl.pallas_call(
        finish_kernel,
        out_shape=f32(rows, width),
        in_specs=[SMEM] + [VMEM] * (5 + len(strips)),
        out_specs=VMEM,
        compiler_params=PARAMS,
        name="finish",
    )(child_map, base, rows_c, rows_o, upper, inverse, *strips)


def solution(mesh):
    return jax.shard_map(
        body,
        mesh=mesh,
        in_specs=(P("col", ("grp", "row")), P("grp", ("row", "col"), None), P()),
        out_specs=P("col", ("grp", "row")),
        check_vma=False,
    )
```

```python
import functools

import jax
import jax.numpy as jnp
from jax import lax
from jax.experimental import pallas as pl
from jax.experimental.pallas import tpu as pltpu
from jax.sharding import PartitionSpec as P

BLK = 128
PIVOTS = 256
OWNER = ("grp", "row")
HIGHEST = lax.Precision.HIGHEST
SUB = 8
VMEM = pl.BlockSpec(memory_space=pltpu.VMEM)
SMEM = pl.BlockSpec(memory_space=pltpu.SMEM)
PARAMS = pltpu.CompilerParams(vmem_limit_bytes=48 * 1024 * 1024)


def f32(*shape):
    return jax.ShapeDtypeStruct(shape, jnp.float32)


def owner_of():
    return lax.axis_index("grp") * lax.axis_size("row") + lax.axis_index("row")


def dot(a, b, ca, cb):
    return lax.dot_general(
        a, b, (((ca,), (cb,)), ((), ())), precision=HIGHEST, preferred_element_type=jnp.float32
    )


def factor_small(cols):
    n = len(cols)
    d = [[cols[k][i] if i >= k else None for k in range(n)] for i in range(n)]
    low = [[None] * n for _ in range(n)]
    inv = [[None] * n for _ in range(n)]
    for k in range(n):
        root = lax.rsqrt(d[k][k])
        root = root * (1.5 - 0.5 * d[k][k] * root * root)
        inv[k][k] = root
        for i in range(k + 1, n):
            low[i][k] = d[i][k] * root
        for i in range(k + 1, n):
            for j in range(k + 1, i + 1):
                d[i][j] = d[i][j] - low[i][k] * low[j][k]
        for j in range(k):
            total = low[k][j] * inv[j][j]
            for m in range(j + 1, k):
                total = total + low[k][m] * inv[m][j]
            inv[k][j] = -root * total
    return inv


def factor_block(groups):
    count = len(groups)
    shape = (SUB, BLK)
    sub = lax.broadcasted_iota(jnp.int32, shape, 0)
    lane = lax.broadcasted_iota(jnp.int32, shape, 1)
    spread_row = lambda v, i: jnp.broadcast_to(v[i : i + 1, :], shape)
    spread_col = lambda v, c: jnp.broadcast_to(v[:, c : c + 1], shape)
    upper, inverse = [], []
    groups = list(groups)
    for b in range(count):
        base = SUB * b
        cur = groups[b]
        here = [spread_col(cur, base + k) for k in range(SUB)]
        inv = factor_small([[spread_row(here[k], i) for i in range(SUB)] for k in range(SUB)])
        inv_col = []
        for k in range(SUB):
            col = jnp.where(sub == k, inv[k][k], 0.0)
            for i in range(k + 1, SUB):
                col = jnp.where(sub == i, inv[i][k], col)
            inv_col.append(col)
        done = inv_col[0] * spread_row(cur, 0)
        for k in range(1, SUB):
            done = done + inv_col[k] * spread_row(cur, k)
        upper.append(jnp.where(lane >= base + sub, done, 0.0))
        kept = done
        for k in range(SUB):
            kept = jnp.where(lane == base + k, inv_col[k], kept)
        inverse.append(jnp.where(lane <= base + sub, kept, 0.0))
        if b + 1 == count:
            break
        inside = (lane >= base) & (lane < base + SUB)
        nxt = groups[b + 1]
        after = [spread_col(nxt, base + k) for k in range(SUB)]
        nxt = jnp.where(inside, 0.0, nxt)
        for i in range(SUB):
            low = after[0] * inv[i][0]
            for k in range(1, i + 1):
                low = low + after[k] * inv[i][k]
            nxt = nxt - low * spread_row(kept, i)
        groups[b + 1] = nxt
        if b + 2 < count:
            change = dot(done[:, base + 2 * SUB :], kept, 0, 0)
            for j in range(b + 2, count):
                at = SUB * (j - b - 2)
                groups[j] = jnp.where(inside, 0.0, groups[j]) - change[at : at + SUB]
    return upper, inverse


def factor_half(source, upper_ref, inverse_ref):
    upper, inverse = factor_block([source[SUB * g : SUB * (g + 1)] for g in range(BLK // SUB)])
    for g in range(BLK // SUB):
        at = slice(SUB * g, SUB * (g + 1))
        upper_ref[at, :] = upper[g]
        inverse_ref[at, :] = inverse[g]


def first_half_kernel(pieces_ref, upper_ref, inverse_ref, side_ref, next_ref, pivot_ref):
    owners, blocks, part, _ = pieces_ref.shape
    for b in range(blocks):
        for k in range(owners):
            at = b * BLK + part * k
            pivot_ref[at : at + part, :] = pieces_ref[k, b]
    factor_half(pivot_ref[:BLK, :BLK], upper_ref, inverse_ref)
    side = dot(inverse_ref[...], pivot_ref[:BLK, BLK:], 1, 0)
    side_ref[...] = side
    next_ref[...] = pivot_ref[BLK:, BLK:] - dot(side, side, 0, 0)


def second_half_kernel(first_ref, side_ref, next_ref, upper_ref, inverse_ref, second_ref):
    factor_half(next_ref[...], upper_ref, second_ref)
    first, second = first_ref[...], second_ref[...]
    inverse_ref[:BLK, :BLK] = first
    inverse_ref[:BLK, BLK:] = jnp.zeros((BLK, BLK), jnp.float32)
    inverse_ref[BLK:, BLK:] = second
    inverse_ref[BLK:, :BLK] = -dot(second, dot(side_ref[...], first, 0, 0), 1, 0)


def split_kernel(map_ref, strip_ref, front_ref, sums_ref, *refs):
    outs, inv_ref = refs[:-1], refs[-1]
    owners, row_blocks, part, width = sums_ref.shape
    per = width // BLK
    grp, row, col = (lax.axis_index(a) for a in ("grp", "row", "col"))
    n_row, n_col = lax.axis_size("row"), lax.axis_size("col")
    me = grp * n_row + row
    for q in range(map_ref.shape[1]):
        inv_ref[map_ref[grp, q]] = q
    mine = map_ref[grp, row * n_col + col] - col * row_blocks
    for s in range(per):
        at = pl.multiple_of(inv_ref[s] * BLK, BLK)
        lanes = slice(s * BLK, (s + 1) * BLK)
        for k in range(owners):
            piece = strip_ref[part * k : part * (k + 1), pl.ds(at, BLK)]
            for b in range(row_blocks):
                rows = slice(b * BLK + part * k, b * BLK + part * (k + 1))
                value = jnp.where(mine == b, piece, 0.0)
                sums_ref[k, b, :, lanes] = value + jnp.where(me == 0, front_ref[rows, lanes], 0.0)
    for d in range(owners):
        for s in range(per):
            at = pl.multiple_of(inv_ref[(me ^ d) * per + s] * BLK, BLK)
            outs[d][:, s * BLK : (s + 1) * BLK] = strip_ref[:, pl.ds(at, BLK)]


def place_rows(target_ref, pieces_ref, grp):
    n_row, blocks, part, _ = pieces_ref.shape
    for b in range(blocks):
        for r in range(n_row):
            at = pl.multiple_of(b * BLK + (grp * n_row + r) * part, SUB)
            target_ref[pl.ds(at, part), :] = pieces_ref[r, b]


def finish_kernel(few, map_ref, front_ref, near_ref, far_ref, upper_ref, side_ref, upper2_ref, inverse_ref, *refs):
    parts, strips, (out_ref, rows_c_ref, rows_o_ref) = refs[: few[0]], refs[few[0] : -3], refs[-3:]
    rows, width = out_ref.shape
    n_row, n_col = lax.axis_size("row"), lax.axis_size("col")
    grp, col = lax.axis_index("grp"), lax.axis_index("col")
    me = owner_of()
    row_blocks = rows // BLK
    inv = inverse_ref[...]
    if few[1]:
        place_rows(rows_c_ref, near_ref, grp)
        place_rows(rows_c_ref, far_ref, 1 - grp)
    else:
        rows_c_ref[...] = near_ref[...]
        rows_o_ref[...] = far_ref[...]
    left = dot(rows_c_ref[...], inv, 1, 1)

    @pl.when(me == 0)
    def _():
        out_ref[...] = left

        @pl.when(col == 0)
        def _():
            out_ref[:BLK, :BLK] = upper_ref[...].T
            out_ref[:BLK, BLK:] = jnp.zeros((BLK, BLK), jnp.float32)
            out_ref[BLK:PIVOTS, :BLK] = side_ref[...].T
            out_ref[BLK:PIVOTS, BLK:] = upper2_ref[...].T

    @pl.when(me != 0)
    def _():
        distance = (me * width // rows) ^ col
        for e, ref in enumerate(parts):

            @pl.when(distance == e)
            def _():
                half = ref.shape[0] // 2
                place_rows(rows_o_ref, ref.at[:half], grp)
                place_rows(rows_o_ref, ref.at[half:], 1 - grp)

        right = dot(rows_o_ref[...], inv, 1, 1)
        out_ref[...] = front_ref[...] - dot(left, right, 1, 1)
        for d, ref in enumerate(strips):
            source = me ^ d
            local = map_ref[source // n_row, source % n_row * n_col + col] - col * row_blocks
            start = pl.multiple_of(local * BLK, BLK)
            out_ref[pl.ds(start, BLK), :] += ref[...]

        @pl.when(col == 0)
        def _():
            out_ref[:PIVOTS, :] = jnp.zeros((PIVOTS, width), jnp.float32)


def from_root(value, axis, root):
    mine = lax.axis_index(axis) == root
    return lax.psum(jnp.where(mine, value, jnp.zeros_like(value)), axis)


def gather_wide(front, strip, child_map):
    n_row, n_col = lax.axis_size("row"), lax.axis_size("col")
    owners = lax.axis_size(OWNER)
    rows, width = front.shape
    row_blocks = rows // BLK
    blocks = owners * width // BLK
    me = owner_of()
    col = lax.axis_index("col")
    hits = child_map[lax.axis_index("grp")][None, :] == jnp.arange(blocks)[:, None]
    source = jnp.argmax(hits, axis=1)
    taken = jnp.take(strip.reshape(BLK, -1, BLK), source, axis=1)
    taken = jnp.where(jnp.any(hits, axis=1)[None, :, None], taken, 0.0)
    outgoing = taken.reshape(BLK, owners, width).transpose(1, 0, 2)
    incoming = lax.all_to_all(outgoing, OWNER, split_axis=0, concat_axis=0, tiled=True)
    ids = jnp.arange(owners)
    places = child_map[ids // n_row, ids % n_row * n_col + col] - col * row_blocks
    assembled = front.reshape(row_blocks, BLK, width).at[places].add(incoming).reshape(rows, width)
    rows_c = from_root(assembled, OWNER, 0)
    pivot = from_root(rows_c[:PIVOTS], "col", 0)
    part = lax.dynamic_slice_in_dim(rows_c, me * width % rows, width, 0)
    rows_o = jnp.zeros((width, width), jnp.float32)
    for c in range(n_col):
        low = c * rows // width
        sent = from_root(part, "col", c)
        rows_o = jnp.where((me >= low) & (me < low + rows // width), sent, rows_o)
    return assembled, rows_c, rows_o, pivot.reshape(1, PIVOTS // BLK, BLK, width), [], []


def spread(piece, axis):
    copies = jnp.broadcast_to(piece[None], (lax.axis_size(axis),) + piece.shape)
    return lax.all_to_all(copies, axis, split_axis=0, concat_axis=0, tiled=True)


def exchange(value, d):
    perm = [(i, i ^ d) for i in range(lax.axis_size(OWNER)) if i != d]
    return lax.ppermute(value, OWNER, perm)


def gather_pieces(front, strip, child_map):
    n_col = lax.axis_size("col")
    owners = lax.axis_size(OWNER)
    rows, width = front.shape
    row_blocks = rows // BLK
    tops = PIVOTS // BLK
    part = BLK // owners
    me = owner_of()
    col = lax.axis_index("col")
    sums, *strips = pl.pallas_call(
        split_kernel,
        out_shape=[f32(owners, row_blocks, part, width)] + [f32(BLK, width)] * owners,
        in_specs=[SMEM, VMEM, VMEM],
        out_specs=[VMEM] * (1 + owners),
        scratch_shapes=[pltpu.SMEM((child_map.shape[1],), jnp.int32)],
        compiler_params=PARAMS,
        name="split",
    )(child_map, strip, front)
    strips = [strips[0]] + [exchange(strips[d], d) for d in range(1, owners)]

    mine = jnp.sum(lax.all_to_all(sums, OWNER, split_axis=0, concat_axis=0, tiled=True), axis=0)
    top = mine[:tops]
    pivot = jnp.where(col == 0, top, 0.0)
    for c in range(1, n_col):
        pivot = pivot + lax.ppermute(top, "col", [(0, c)])
    pivot = spread(pivot, OWNER)
    mine, pivot = lax.optimization_barrier((mine, pivot))
    near = spread(mine, "row")
    far = lax.ppermute(near, "grp", [(0, 1), (1, 0)])

    at = me * width % rows // BLK
    cut = lambda v: lax.dynamic_slice_in_dim(v, at, width // BLK, 1)
    own_part = jnp.concatenate([cut(near), cut(far)], axis=0)
    parts = [own_part]
    for e in range(1, n_col):
        perm = []
        for o in range(owners):
            c = o * width // rows
            perm.append((o * n_col + c, o * n_col + (c ^ e)))
        parts.append(lax.ppermute(own_part, OWNER + ("col",), perm))
    return front, near, far, pivot, parts, strips


def body(front, child_blocks, child_map):
    owners = lax.axis_size(OWNER)
    rows, width = front.shape
    blocks = owners * width // BLK
    few = lax.axis_size("grp") == 2 and BLK % (owners * 8) == 0 and child_map.shape[1] == blocks
    gather = gather_pieces if few else gather_wide
    base, near, far, pivot, parts, strips = gather(front, child_blocks[0], child_map)
    half = f32(BLK, BLK)
    cost = pl.CostEstimate(flops=8_000_000_000, bytes_accessed=1 << 18, transcendentals=0)
    upper, first, side, rest = pl.pallas_call(
        first_half_kernel,
        out_shape=[half] * 4,
        in_specs=[VMEM],
        out_specs=[VMEM] * 4,
        scratch_shapes=[pltpu.VMEM((PIVOTS, PIVOTS), jnp.float32)],
        compiler_params=PARAMS,
        cost_estimate=cost,
        name="pivot_first",
    )(pivot)
    upper2, inverse = pl.pallas_call(
        second_half_kernel,
        out_shape=[half, f32(PIVOTS, PIVOTS)],
        in_specs=[VMEM] * 3,
        out_specs=[VMEM] * 2,
        scratch_shapes=[pltpu.VMEM((BLK, BLK), jnp.float32)],
        compiler_params=PARAMS,
        cost_estimate=cost,
        name="pivot_second",
    )(first, side, rest)
    return pl.pallas_call(
        functools.partial(finish_kernel, (len(parts), few)),
        out_shape=f32(rows, width),
        in_specs=[SMEM] + [VMEM] * (7 + len(parts) + len(strips)),
        out_specs=VMEM,
        scratch_shapes=[pltpu.VMEM((rows, width), jnp.float32), pltpu.VMEM((width, width), jnp.float32)],
        compiler_params=PARAMS,
        name="finish",
    )(child_map, base, near, far, upper, side, upper2, inverse, *parts, *strips)


def solution(mesh):
    return jax.shard_map(
        body,
        mesh=mesh,
        in_specs=(P("col", ("grp", "row")), P("grp", ("row", "col"), None), P()),
        out_specs=P("col", ("grp", "row")),
        check_vma=False,
    )
```

```python
import functools

import jax
import jax.numpy as jnp
from jax import lax
from jax.experimental import pallas as pl
from jax.experimental.pallas import tpu as pltpu
from jax.sharding import PartitionSpec as P

BLK = 128
PIVOTS = 256
OWNER = ("grp", "row")
HIGHEST = lax.Precision.HIGHEST
SUB = 8
VMEM = pl.BlockSpec(memory_space=pltpu.VMEM)
SMEM = pl.BlockSpec(memory_space=pltpu.SMEM)
PARAMS = pltpu.CompilerParams(vmem_limit_bytes=48 * 1024 * 1024)


def f32(*shape):
    return jax.ShapeDtypeStruct(shape, jnp.float32)


def owner_of():
    return lax.axis_index("grp") * lax.axis_size("row") + lax.axis_index("row")


def dot(a, b, ca, cb):
    return lax.dot_general(
        a, b, (((ca,), (cb,)), ((), ())), precision=HIGHEST, preferred_element_type=jnp.float32
    )


def factor_small(cols):
    n = len(cols)
    d = [[cols[k][i] if i >= k else None for k in range(n)] for i in range(n)]
    low = [[None] * n for _ in range(n)]
    inv = [[None] * n for _ in range(n)]
    for k in range(n):
        root = lax.rsqrt(d[k][k])
        root = root * (1.5 - 0.5 * d[k][k] * root * root)
        inv[k][k] = root
        for i in range(k + 1, n):
            low[i][k] = d[i][k] * root
        for i in range(k + 1, n):
            for j in range(k + 1, i + 1):
                d[i][j] = d[i][j] - low[i][k] * low[j][k]
        for j in range(k):
            total = low[k][j] * inv[j][j]
            for m in range(j + 1, k):
                total = total + low[k][m] * inv[m][j]
            inv[k][j] = -root * total
    return inv


def factor_block(groups):
    count = len(groups)
    shape = (SUB, BLK)
    sub = lax.broadcasted_iota(jnp.int32, shape, 0)
    lane = lax.broadcasted_iota(jnp.int32, shape, 1)
    spread_row = lambda v, i: jnp.broadcast_to(v[i : i + 1, :], shape)
    spread_col = lambda v, c: jnp.broadcast_to(v[:, c : c + 1], shape)
    upper, inverse = [], []
    groups = list(groups)
    for b in range(count):
        base = SUB * b
        cur = groups[b]
        here = [spread_col(cur, base + k) for k in range(SUB)]
        inv = factor_small([[spread_row(here[k], i) for i in range(SUB)] for k in range(SUB)])
        inv_col = []
        for k in range(SUB):
            col = jnp.where(sub == k, inv[k][k], 0.0)
            for i in range(k + 1, SUB):
                col = jnp.where(sub == i, inv[i][k], col)
            inv_col.append(col)
        done = inv_col[0] * spread_row(cur, 0)
        for k in range(1, SUB):
            done = done + inv_col[k] * spread_row(cur, k)
        upper.append(jnp.where(lane >= base + sub, done, 0.0))
        kept = done
        for k in range(SUB):
            kept = jnp.where(lane == base + k, inv_col[k], kept)
        inverse.append(jnp.where(lane <= base + sub, kept, 0.0))
        if b + 1 == count:
            break
        inside = (lane >= base) & (lane < base + SUB)
        nxt = groups[b + 1]
        after = [spread_col(nxt, base + k) for k in range(SUB)]
        nxt = jnp.where(inside, 0.0, nxt)
        for i in range(SUB):
            low = after[0] * inv[i][0]
            for k in range(1, i + 1):
                low = low + after[k] * inv[i][k]
            nxt = nxt - low * spread_row(kept, i)
        groups[b + 1] = nxt
        if b + 2 < count:
            change = dot(done[:, base + 2 * SUB :], kept, 0, 0)
            for j in range(b + 2, count):
                at = SUB * (j - b - 2)
                groups[j] = jnp.where(inside, 0.0, groups[j]) - change[at : at + SUB]
    return upper, inverse


def factor_half(source, upper_ref, inverse_ref):
    upper, inverse = factor_block([source[SUB * g : SUB * (g + 1)] for g in range(BLK // SUB)])
    for g in range(BLK // SUB):
        at = slice(SUB * g, SUB * (g + 1))
        upper_ref[at, :] = upper[g]
        inverse_ref[at, :] = inverse[g]


def on_root(few):
    return lax.axis_index("col") == 0 if few else lax.axis_index("col") >= 0


def first_half_kernel(few, *refs):
    sources, (upper_ref, inverse_ref, side_ref, next_ref, pivot_ref) = refs[:-5], refs[-5:]

    @pl.when(on_root(few))
    def _():
        if few:
            grp = lax.axis_index("grp")
            tops = PIVOTS // BLK
            place_rows(pivot_ref, sources[0].at[:, :tops], grp)
            place_rows(pivot_ref, sources[1].at[:, :tops], 1 - grp)
        else:
            pivot_ref[...] = sources[0][...]
        factor_half(pivot_ref[:BLK, :BLK], upper_ref, inverse_ref)
        side = dot(inverse_ref[...], pivot_ref[:BLK, BLK:], 1, 0)
        side_ref[...] = side
        next_ref[...] = pivot_ref[BLK:, BLK:] - dot(side, side, 0, 0)


def second_half_kernel(few, first_ref, side_ref, next_ref, upper_ref, inverse_ref, second_ref):
    @pl.when(on_root(few))
    def _():
        factor_half(next_ref[...], upper_ref, second_ref)
        first, second = first_ref[...], second_ref[...]
        inverse_ref[:BLK, :BLK] = first
        inverse_ref[:BLK, BLK:] = jnp.zeros((BLK, BLK), jnp.float32)
        inverse_ref[BLK:, BLK:] = second
        inverse_ref[BLK:, :BLK] = -dot(second, dot(side_ref[...], first, 0, 0), 1, 0)


def split_kernel(map_ref, strip_hbm, front_hbm, sums_ref, out_ref, inv_ref, strip_ref, front_ref, sems):
    owners, row_blocks, part, width = sums_ref.shape
    per = width // BLK
    grp, row, col = (lax.axis_index(a) for a in ("grp", "row", "col"))
    n_row, n_col = lax.axis_size("row"), lax.axis_size("col")
    me = grp * n_row + row
    get_strip = pltpu.make_async_copy(strip_hbm, strip_ref, sems.at[0])
    get_front = pltpu.make_async_copy(front_hbm, front_ref, sems.at[1])
    get_strip.start()

    @pl.when(me == 0)
    def _():
        get_front.start()

    for q in range(map_ref.shape[1]):
        inv_ref[map_ref[grp, q]] = q
    mine = map_ref[grp, row * n_col + col] - col * row_blocks
    get_strip.wait()
    for s in range(per):
        at = pl.multiple_of(inv_ref[s] * BLK, BLK)
        lanes = slice(s * BLK, (s + 1) * BLK)
        for k in range(owners):
            piece = strip_ref[part * k : part * (k + 1), pl.ds(at, BLK)]
            for b in range(row_blocks):
                sums_ref[k, b, :, lanes] = jnp.where(mine == b, piece, 0.0)

    @pl.when(me == 0)
    def _():
        get_front.wait()
        for k in range(owners):
            for b in range(row_blocks):
                at = b * BLK + part * k
                sums_ref[k, b] = sums_ref[k, b] + front_ref[at : at + part, :]

    for k in range(owners):
        for s in range(per):
            at = pl.multiple_of(inv_ref[k * per + s] * BLK, BLK)
            out_ref[k, :, s * BLK : (s + 1) * BLK] = strip_ref[:, pl.ds(at, BLK)]


def place_rows(target_ref, pieces_ref, grp):
    n_row, blocks, part, _ = pieces_ref.shape
    for b in range(blocks):
        for r in range(n_row):
            at = pl.multiple_of(b * BLK + (grp * n_row + r) * part, SUB)
            target_ref[pl.ds(at, part), :] = pieces_ref[r, b]


def choose(refs, distance, take):
    for ref, here in zip(refs, (distance == 0, distance == 2, distance % 2 == 1)):
        pl.when(here)(functools.partial(take, ref))


def finish_kernel(few, map_ref, front_ref, near_ref, far_ref, upper_ref, side_ref, upper2_ref, *refs):
    count = 3 if few else 1
    inverses, parts, strips = refs[:count], refs[count : 2 * count], refs[2 * count : -4]
    out_ref, rows_c_ref, rows_o_ref, inv_ref = refs[-4:]
    rows, width = out_ref.shape
    n_row, n_col = lax.axis_size("row"), lax.axis_size("col")
    grp, col = lax.axis_index("grp"), lax.axis_index("col")
    me = owner_of()
    row_blocks = rows // BLK

    def take_inverse(ref):
        inv_ref[...] = ref[...]

    def take_part(ref):
        half = ref.shape[0] // 2
        place_rows(rows_o_ref, ref.at[:half], grp)
        place_rows(rows_o_ref, ref.at[half:], 1 - grp)

    if few:
        choose(inverses, col, take_inverse)
        choose(parts, (me * width // rows) ^ col, take_part)
        place_rows(rows_c_ref, near_ref, grp)
        place_rows(rows_c_ref, far_ref, 1 - grp)
    else:
        inv_ref[...] = inverses[0][...]
        rows_o_ref[...] = parts[0][...]
        rows_c_ref[...] = near_ref[...]
    inv = inv_ref[...]
    left = dot(rows_c_ref[...], inv, 1, 1)

    @pl.when(me == 0)
    def _():
        out_ref[...] = left

        @pl.when(col == 0)
        def _():
            out_ref[:BLK, :BLK] = upper_ref[...].T
            out_ref[:BLK, BLK:] = jnp.zeros((BLK, BLK), jnp.float32)
            out_ref[BLK:PIVOTS, :BLK] = side_ref[...].T
            out_ref[BLK:PIVOTS, BLK:] = upper2_ref[...].T

    @pl.when(me != 0)
    def _():
        right = dot(rows_o_ref[...], inv, 1, 1)
        out_ref[...] = front_ref[...] - dot(left, right, 1, 1)
        for ref in strips:
            for i in range(ref.shape[0]):
                local = map_ref[i // n_row, i % n_row * n_col + col] - col * row_blocks
                start = pl.multiple_of(local * BLK, BLK)
                out_ref[pl.ds(start, BLK), :] += ref[i]

        @pl.when(col == 0)
        def _():
            out_ref[:PIVOTS, :] = jnp.zeros((PIVOTS, width), jnp.float32)


def from_root(value, axis, root):
    mine = lax.axis_index(axis) == root
    return lax.psum(jnp.where(mine, value, jnp.zeros_like(value)), axis)


def gather_wide(front, strip, child_map):
    n_row, n_col = lax.axis_size("row"), lax.axis_size("col")
    owners = lax.axis_size(OWNER)
    rows, width = front.shape
    row_blocks = rows // BLK
    blocks = owners * width // BLK
    me = owner_of()
    col = lax.axis_index("col")
    hits = child_map[lax.axis_index("grp")][None, :] == jnp.arange(blocks)[:, None]
    source = jnp.argmax(hits, axis=1)
    taken = jnp.take(strip.reshape(BLK, -1, BLK), source, axis=1)
    taken = jnp.where(jnp.any(hits, axis=1)[None, :, None], taken, 0.0)
    outgoing = taken.reshape(BLK, owners, width).transpose(1, 0, 2)
    incoming = lax.all_to_all(outgoing, OWNER, split_axis=0, concat_axis=0, tiled=True)
    ids = jnp.arange(owners)
    places = child_map[ids // n_row, ids % n_row * n_col + col] - col * row_blocks
    assembled = front.reshape(row_blocks, BLK, width).at[places].add(incoming).reshape(rows, width)
    rows_c = from_root(assembled, OWNER, 0)
    pivot = from_root(rows_c[:PIVOTS], "col", 0)
    part = lax.dynamic_slice_in_dim(rows_c, me * width % rows, width, 0)
    rows_o = jnp.zeros((width, width), jnp.float32)
    for c in range(n_col):
        low = c * rows // width
        sent = from_root(part, "col", c)
        rows_o = jnp.where((me >= low) & (me < low + rows // width), sent, rows_o)
    return assembled, (rows_c, rows_c), [rows_o], [pivot], []


def spread(piece, axis):
    copies = jnp.broadcast_to(piece[None], (lax.axis_size(axis),) + piece.shape)
    return lax.all_to_all(copies, axis, split_axis=0, concat_axis=0, tiled=True)


def over_col(value, roots):
    n_col = lax.axis_size("col")
    axes = OWNER + ("col",)
    cross = [(o * n_col + c, o * n_col + (c ^ 2)) for o, c in enumerate(roots)]
    over_x = lax.ppermute(value, axes, cross)
    held = jnp.where(lax.axis_index("col") == jnp.array(roots)[owner_of()], value, over_x)
    other = [(o * n_col + (c ^ e), o * n_col + (c ^ e ^ 1)) for o, c in enumerate(roots) for e in (0, 2)]
    return [value, over_x, lax.ppermute(held, axes, other)]


def gather_pieces(front, strip, child_map):
    owners = lax.axis_size(OWNER)
    rows, width = front.shape
    row_blocks = rows // BLK
    part = BLK // owners
    me = owner_of()
    any_space = pl.BlockSpec(memory_space=pl.ANY)
    sums, strips = pl.pallas_call(
        split_kernel,
        out_shape=[f32(owners, row_blocks, part, width), f32(owners, BLK, width)],
        in_specs=[SMEM, any_space, any_space],
        out_specs=[VMEM] * 2,
        scratch_shapes=[
            pltpu.SMEM((child_map.shape[1],), jnp.int32),
            pltpu.VMEM(strip.shape, jnp.float32),
            pltpu.VMEM(front.shape, jnp.float32),
            pltpu.SemaphoreType.DMA((2,)),
        ],
        compiler_params=PARAMS,
        name="split",
    )(child_map, strip, front)
    mine = jnp.sum(lax.all_to_all(sums, OWNER, split_axis=0, concat_axis=0, tiled=True), axis=0)
    near = spread(mine, "row")
    strips, near = lax.optimization_barrier((strips, near))
    strips = lax.all_to_all(strips, OWNER, split_axis=0, concat_axis=0, tiled=True)
    far = lax.ppermute(near, "grp", [(0, 1), (1, 0)])

    at = me * width % rows // BLK
    cut = lambda v: lax.dynamic_slice_in_dim(v, at, width // BLK, 1)
    own_part = jnp.concatenate([cut(near), cut(far)], axis=0)
    parts = over_col(own_part, [o * width // rows for o in range(owners)])
    return front, (near, far), parts, [near, far], [strips]


def body(front, child_blocks, child_map):
    owners = lax.axis_size(OWNER)
    rows, width = front.shape
    blocks = owners * width // BLK
    few = lax.axis_size("grp") == 2 and lax.axis_size("col") == 4
    few = few and BLK % (owners * 8) == 0 and child_map.shape[1] == blocks
    gather = gather_pieces if few else gather_wide
    base, panel, parts, pivot, strips = gather(front, child_blocks[0], child_map)
    half = f32(BLK, BLK)
    cost = pl.CostEstimate(flops=8_000_000_000, bytes_accessed=1 << 18, transcendentals=0)
    upper, first, side, rest = pl.pallas_call(
        functools.partial(first_half_kernel, few),
        out_shape=[half] * 4,
        in_specs=[VMEM] * len(pivot),
        out_specs=[VMEM] * 4,
        scratch_shapes=[pltpu.VMEM((PIVOTS, PIVOTS), jnp.float32)],
        compiler_params=PARAMS,
        cost_estimate=cost,
        name="pivot_first",
    )(*pivot)
    upper2, inverse = pl.pallas_call(
        functools.partial(second_half_kernel, few),
        out_shape=[half, f32(PIVOTS, PIVOTS)],
        in_specs=[VMEM] * 3,
        out_specs=[VMEM] * 2,
        scratch_shapes=[pltpu.VMEM((BLK, BLK), jnp.float32)],
        compiler_params=PARAMS,
        cost_estimate=cost,
        name="pivot_second",
    )(first, side, rest)
    inverses = over_col(inverse, [0] * owners) if few else [inverse]
    return pl.pallas_call(
        functools.partial(finish_kernel, few),
        out_shape=f32(rows, width),
        in_specs=[SMEM] + [VMEM] * (6 + len(inverses) + len(parts) + len(strips)),
        out_specs=VMEM,
        scratch_shapes=[pltpu.VMEM((n, width), jnp.float32) for n in (rows, width, PIVOTS)],
        compiler_params=PARAMS,
        name="finish",
    )(child_map, base, *panel, upper, side, upper2, *inverses, *parts, *strips)


def solution(mesh):
    return jax.shard_map(
        body,
        mesh=mesh,
        in_specs=(P("col", ("grp", "row")), P("grp", ("row", "col"), None), P()),
        out_specs=P("col", ("grp", "row")),
        check_vma=False,
    )
```

```python
import functools

import jax
import jax.numpy as jnp
from jax import lax
from jax.experimental import pallas as pl
from jax.experimental.pallas import tpu as pltpu
from jax.sharding import PartitionSpec as P

BLK = 128
PIVOTS = 256
OWNER = ("grp", "row")
HIGHEST = lax.Precision.HIGHEST
SUB = 8
VMEM = pl.BlockSpec(memory_space=pltpu.VMEM)
SMEM = pl.BlockSpec(memory_space=pltpu.SMEM)
PARAMS = pltpu.CompilerParams(vmem_limit_bytes=48 * 1024 * 1024)


def f32(*shape):
    return jax.ShapeDtypeStruct(shape, jnp.float32)


def owner_of():
    return lax.axis_index("grp") * lax.axis_size("row") + lax.axis_index("row")


def dot(a, b, ca, cb):
    return lax.dot_general(
        a, b, (((ca,), (cb,)), ((), ())), precision=HIGHEST, preferred_element_type=jnp.float32
    )


def factor_small(cols):
    n = len(cols)
    d = [[cols[k][i] if i >= k else None for k in range(n)] for i in range(n)]
    low = [[None] * n for _ in range(n)]
    inv = [[None] * n for _ in range(n)]
    for k in range(n):
        root = lax.rsqrt(d[k][k])
        inv[k][k] = root
        for i in range(k + 1, n):
            low[i][k] = d[i][k] * root
        for i in range(k + 1, n):
            for j in range(k + 1, i + 1):
                d[i][j] = d[i][j] - low[i][k] * low[j][k]
        for j in range(k):
            total = low[k][j] * inv[j][j]
            for m in range(j + 1, k):
                total = total + low[k][m] * inv[m][j]
            inv[k][j] = -root * total
    return inv


def factor_block(groups):
    count = len(groups)
    shape = (SUB, BLK)
    sub = lax.broadcasted_iota(jnp.int32, shape, 0)
    lane = lax.broadcasted_iota(jnp.int32, shape, 1)
    spread_row = lambda v, i: jnp.broadcast_to(v[i : i + 1, :], shape)
    spread_col = lambda v, c: jnp.broadcast_to(v[:, c : c + 1], shape)
    upper, inverse = [], []
    groups = list(groups)
    for b in range(count):
        base = SUB * b
        cur = groups[b]
        here = [spread_col(cur, base + k) for k in range(SUB)]
        inv = factor_small([[spread_row(here[k], i) for i in range(SUB)] for k in range(SUB)])
        inv_col = []
        for k in range(SUB):
            col = jnp.where(sub == k, inv[k][k], 0.0)
            for i in range(k + 1, SUB):
                col = jnp.where(sub == i, inv[i][k], col)
            inv_col.append(col)
        done = inv_col[0] * spread_row(cur, 0)
        for k in range(1, SUB):
            done = done + inv_col[k] * spread_row(cur, k)
        upper.append(jnp.where(lane >= base + sub, done, 0.0))
        kept = done
        for k in range(SUB):
            kept = jnp.where(lane == base + k, inv_col[k], kept)
        inverse.append(jnp.where(lane <= base + sub, kept, 0.0))
        if b + 1 == count:
            break
        inside = (lane >= base) & (lane < base + SUB)
        nxt = groups[b + 1]
        after = [spread_col(nxt, base + k) for k in range(SUB)]
        nxt = jnp.where(inside, 0.0, nxt)
        for i in range(SUB):
            low = after[0] * inv[i][0]
            for k in range(1, i + 1):
                low = low + after[k] * inv[i][k]
            nxt = nxt - low * spread_row(kept, i)
        groups[b + 1] = nxt
        if b + 2 < count:
            change = dot(done[:, base + 2 * SUB :], kept, 0, 0)
            for j in range(b + 2, count):
                at = SUB * (j - b - 2)
                groups[j] = jnp.where(inside, 0.0, groups[j]) - change[at : at + SUB]
    return upper, inverse


def factor_half(source, upper_ref, inverse_ref):
    upper, inverse = factor_block([source[SUB * g : SUB * (g + 1)] for g in range(BLK // SUB)])
    for g in range(BLK // SUB):
        at = slice(SUB * g, SUB * (g + 1))
        upper_ref[at, :] = upper[g]
        inverse_ref[at, :] = inverse[g]


def on_root(few):
    return lax.axis_index("col") == 0 if few else lax.axis_index("col") >= 0


def first_half_kernel(few, *refs):
    sources, (upper_ref, inverse_ref, side_ref, next_ref, pivot_ref) = refs[:-5], refs[-5:]

    @pl.when(on_root(few))
    def _():
        if few:
            grp = lax.axis_index("grp")
            tops = PIVOTS // BLK
            place_rows(pivot_ref, sources[0].at[:, :tops], grp)
            place_rows(pivot_ref, sources[1].at[:, :tops], 1 - grp)
        else:
            pivot_ref[...] = sources[0][...]
        factor_half(pivot_ref[:BLK, :BLK], upper_ref, inverse_ref)
        side = dot(inverse_ref[...], pivot_ref[:BLK, BLK:], 1, 0)
        side_ref[...] = side
        next_ref[...] = pivot_ref[BLK:, BLK:] - dot(side, side, 0, 0)


def second_half_kernel(few, first_ref, side_ref, next_ref, upper_ref, inverse_ref, second_ref):
    @pl.when(on_root(few))
    def _():
        factor_half(next_ref[...], upper_ref, second_ref)
        first, second = first_ref[...], second_ref[...]
        inverse_ref[:BLK, :BLK] = first
        inverse_ref[:BLK, BLK:] = jnp.zeros((BLK, BLK), jnp.float32)
        inverse_ref[BLK:, BLK:] = second
        inverse_ref[BLK:, :BLK] = -dot(second, dot(side_ref[...], first, 0, 0), 1, 0)


def split_kernel(map_ref, strip_hbm, front_hbm, sums_ref, out_ref, inv_ref, strip_ref, front_ref, sems):
    owners, row_blocks, part, width = sums_ref.shape
    per = width // BLK
    grp, row, col = (lax.axis_index(a) for a in ("grp", "row", "col"))
    n_row, n_col = lax.axis_size("row"), lax.axis_size("col")
    me = grp * n_row + row
    get_strip = pltpu.make_async_copy(strip_hbm, strip_ref, sems.at[0])
    get_front = pltpu.make_async_copy(front_hbm, front_ref, sems.at[1])
    get_strip.start()

    @pl.when(me == 0)
    def _():
        get_front.start()

    for q in range(map_ref.shape[1]):
        inv_ref[map_ref[grp, q]] = q
    mine = map_ref[grp, row * n_col + col] - col * row_blocks
    get_strip.wait()
    for s in range(per):
        at = pl.multiple_of(inv_ref[s] * BLK, BLK)
        lanes = slice(s * BLK, (s + 1) * BLK)
        for k in range(owners):
            piece = strip_ref[part * k : part * (k + 1), pl.ds(at, BLK)]
            for b in range(row_blocks):
                sums_ref[k, b, :, lanes] = jnp.where(mine == b, piece, 0.0)

    @pl.when(me == 0)
    def _():
        get_front.wait()
        for k in range(owners):
            for b in range(row_blocks):
                at = b * BLK + part * k
                sums_ref[k, b] = sums_ref[k, b] + front_ref[at : at + part, :]

    for k in range(owners):
        for s in range(per):
            at = pl.multiple_of(inv_ref[k * per + s] * BLK, BLK)
            out_ref[k, :, s * BLK : (s + 1) * BLK] = strip_ref[:, pl.ds(at, BLK)]


def place_rows(target_ref, pieces_ref, grp):
    n_row, blocks, part, _ = pieces_ref.shape
    for b in range(blocks):
        for r in range(n_row):
            at = pl.multiple_of(b * BLK + (grp * n_row + r) * part, SUB)
            target_ref[pl.ds(at, part), :] = pieces_ref[r, b]


def choose(refs, distance, take):
    for ref, here in zip(refs, (distance == 0, distance == 2, distance % 2 == 1)):
        pl.when(here)(functools.partial(take, ref))


def assemble_kernel(map_ref, front_ref, strips_ref, out_ref):
    n_row, n_col = lax.axis_size("row"), lax.axis_size("col")
    col = lax.axis_index("col")
    row_blocks = out_ref.shape[0] // BLK
    out_ref[...] = front_ref[...]
    for i in range(strips_ref.shape[0]):
        local = map_ref[i // n_row, i % n_row * n_col + col] - col * row_blocks
        start = pl.multiple_of(local * BLK, BLK)
        out_ref[pl.ds(start, BLK), :] += strips_ref[i]


def finish_kernel(few, base_ref, near_ref, far_ref, upper_ref, side_ref, upper2_ref, *refs):
    count = 3 if few else 1
    inverses, parts = refs[:count], refs[count : 2 * count]
    out_ref, rows_c_ref, rows_o_ref, inv_ref = refs[-4:]
    rows, width = out_ref.shape
    grp, col = lax.axis_index("grp"), lax.axis_index("col")
    me = owner_of()

    def take_inverse(ref):
        inv_ref[...] = ref[...]

    def take_part(ref):
        half = ref.shape[0] // 2
        place_rows(rows_o_ref, ref.at[:half], grp)
        place_rows(rows_o_ref, ref.at[half:], 1 - grp)

    if few:
        choose(inverses, col, take_inverse)
        choose(parts, (me * width // rows) ^ col, take_part)
        place_rows(rows_c_ref, near_ref, grp)
        place_rows(rows_c_ref, far_ref, 1 - grp)
    else:
        inv_ref[...] = inverses[0][...]
        rows_o_ref[...] = parts[0][...]
        rows_c_ref[...] = near_ref[...]
    inv = inv_ref[...]
    left = dot(rows_c_ref[...], inv, 1, 1)

    @pl.when(me == 0)
    def _():
        out_ref[...] = left

        @pl.when(col == 0)
        def _():
            out_ref[:BLK, :BLK] = upper_ref[...].T
            out_ref[:BLK, BLK:] = jnp.zeros((BLK, BLK), jnp.float32)
            out_ref[BLK:PIVOTS, :BLK] = side_ref[...].T
            out_ref[BLK:PIVOTS, BLK:] = upper2_ref[...].T

    @pl.when(me != 0)
    def _():
        right = dot(rows_o_ref[...], inv, 1, 1)
        out_ref[...] = base_ref[...] - dot(left, right, 1, 1)

        @pl.when(col == 0)
        def _():
            out_ref[:PIVOTS, :] = jnp.zeros((PIVOTS, width), jnp.float32)


def from_root(value, axis, root):
    mine = lax.axis_index(axis) == root
    return lax.psum(jnp.where(mine, value, jnp.zeros_like(value)), axis)


def gather_wide(front, strip, child_map):
    n_row, n_col = lax.axis_size("row"), lax.axis_size("col")
    owners = lax.axis_size(OWNER)
    rows, width = front.shape
    row_blocks = rows // BLK
    blocks = owners * width // BLK
    me = owner_of()
    col = lax.axis_index("col")
    hits = child_map[lax.axis_index("grp")][None, :] == jnp.arange(blocks)[:, None]
    source = jnp.argmax(hits, axis=1)
    taken = jnp.take(strip.reshape(BLK, -1, BLK), source, axis=1)
    taken = jnp.where(jnp.any(hits, axis=1)[None, :, None], taken, 0.0)
    outgoing = taken.reshape(BLK, owners, width).transpose(1, 0, 2)
    incoming = lax.all_to_all(outgoing, OWNER, split_axis=0, concat_axis=0, tiled=True)
    ids = jnp.arange(owners)
    places = child_map[ids // n_row, ids % n_row * n_col + col] - col * row_blocks
    assembled = front.reshape(row_blocks, BLK, width).at[places].add(incoming).reshape(rows, width)
    rows_c = from_root(assembled, OWNER, 0)
    pivot = from_root(rows_c[:PIVOTS], "col", 0)
    part = lax.dynamic_slice_in_dim(rows_c, me * width % rows, width, 0)
    rows_o = jnp.zeros((width, width), jnp.float32)
    for c in range(n_col):
        low = c * rows // width
        sent = from_root(part, "col", c)
        rows_o = jnp.where((me >= low) & (me < low + rows // width), sent, rows_o)
    return assembled, (rows_c, rows_c), [pivot], rows_o


def spread(piece, axis):
    copies = jnp.broadcast_to(piece[None], (lax.axis_size(axis),) + piece.shape)
    return lax.all_to_all(copies, axis, split_axis=0, concat_axis=0, tiled=True)


def over_col(value, roots):
    n_col = lax.axis_size("col")
    axes = OWNER + ("col",)
    cross = [(o * n_col + c, o * n_col + (c ^ 2)) for o, c in enumerate(roots)]
    over_x = lax.ppermute(value, axes, cross)
    held = jnp.where(lax.axis_index("col") == jnp.array(roots)[owner_of()], value, over_x)
    other = [(o * n_col + (c ^ e), o * n_col + (c ^ e ^ 1)) for o, c in enumerate(roots) for e in (0, 2)]
    return [value, over_x, lax.ppermute(held, axes, other)], held


def gather_pieces(front, strip, child_map):
    owners = lax.axis_size(OWNER)
    rows, width = front.shape
    row_blocks = rows // BLK
    part = BLK // owners
    in_hbm = pl.BlockSpec(memory_space=pltpu.HBM)
    sums, strips = pl.pallas_call(
        split_kernel,
        out_shape=[f32(owners, row_blocks, part, width), f32(owners, BLK, width)],
        in_specs=[SMEM, in_hbm, in_hbm],
        out_specs=[VMEM] * 2,
        scratch_shapes=[
            pltpu.SMEM((child_map.shape[1],), jnp.int32),
            pltpu.VMEM(strip.shape, jnp.float32),
            pltpu.VMEM(front.shape, jnp.float32),
            pltpu.SemaphoreType.DMA((2,)),
        ],
        compiler_params=PARAMS,
        name="split",
    )(child_map, strip, front)
    mine = jnp.sum(lax.all_to_all(sums, OWNER, split_axis=0, concat_axis=0, tiled=True), axis=0)
    near = spread(mine, "row")
    strips, near = lax.optimization_barrier((strips, near))
    strips = lax.all_to_all(strips, OWNER, split_axis=0, concat_axis=0, tiled=True)
    far = lax.ppermute(near, "grp", [(0, 1), (1, 0)])

    return front, (near, far), [near, far], strips


def body(front, child_blocks, child_map):
    owners = lax.axis_size(OWNER)
    rows, width = front.shape
    blocks = owners * width // BLK
    few = lax.axis_size("grp") == 2 and lax.axis_size("col") == 4
    few = few and BLK % (owners * 8) == 0 and child_map.shape[1] == blocks
    gather = gather_pieces if few else gather_wide
    base, panel, pivot, last = gather(front, child_blocks[0], child_map)
    half = f32(BLK, BLK)
    cost = pl.CostEstimate(flops=8_000_000_000, bytes_accessed=1 << 18, transcendentals=0)
    upper, first, side, rest = pl.pallas_call(
        functools.partial(first_half_kernel, few),
        out_shape=[half] * 4,
        in_specs=[VMEM] * len(pivot),
        out_specs=[VMEM] * 4,
        scratch_shapes=[pltpu.VMEM((PIVOTS, PIVOTS), jnp.float32)],
        compiler_params=PARAMS,
        cost_estimate=cost,
        name="pivot_first",
    )(*pivot)
    if few:
        first, near, far = lax.optimization_barrier((first, *panel))
        at = owner_of() * width % rows // BLK
        cut = lambda v: lax.dynamic_slice_in_dim(v, at, width // BLK, 1)
        own_part = jnp.concatenate([cut(near), cut(far)], axis=0)
        parts, _ = over_col(own_part, [o * width // rows for o in range(owners)])
    upper2, inverse = pl.pallas_call(
        functools.partial(second_half_kernel, few),
        out_shape=[half, f32(PIVOTS, PIVOTS)],
        in_specs=[VMEM] * 3,
        out_specs=[VMEM] * 2,
        scratch_shapes=[pltpu.VMEM((BLK, BLK), jnp.float32)],
        compiler_params=PARAMS,
        cost_estimate=cost,
        name="pivot_second",
    )(first, side, rest)
    if few:
        inverses, held = over_col(inverse, [0] * owners)
        strips, _ = lax.optimization_barrier((last, held))
        base = pl.pallas_call(
            assemble_kernel,
            out_shape=f32(rows, width),
            in_specs=[SMEM, VMEM, VMEM],
            out_specs=VMEM,
            compiler_params=PARAMS,
            name="assemble",
        )(child_map, base, strips)
    else:
        inverses, parts = [inverse], [last]
    return pl.pallas_call(
        functools.partial(finish_kernel, few),
        out_shape=f32(rows, width),
        in_specs=[VMEM] * (6 + len(inverses) + len(parts)),
        out_specs=VMEM,
        scratch_shapes=[pltpu.VMEM((n, width), jnp.float32) for n in (rows, width, PIVOTS)],
        compiler_params=PARAMS,
        name="finish",
    )(base, *panel, upper, side, upper2, *inverses, *parts)


def solution(mesh):
    return jax.shard_map(
        body,
        mesh=mesh,
        in_specs=(P("col", ("grp", "row")), P("grp", ("row", "col"), None), P()),
        out_specs=P("col", ("grp", "row")),
        check_vma=False,
    )
```

```python
import functools

import jax
import jax.numpy as jnp
from jax import lax
from jax.experimental import pallas as pl
from jax.experimental.pallas import tpu as pltpu
from jax.sharding import PartitionSpec as P

BLK = 128
PIVOTS = 256
OWNER = ("grp", "row")
HIGHEST = lax.Precision.HIGHEST
SUB = 8
VMEM = pl.BlockSpec(memory_space=pltpu.VMEM)
SMEM = pl.BlockSpec(memory_space=pltpu.SMEM)
PARAMS = pltpu.CompilerParams(vmem_limit_bytes=48 * 1024 * 1024)


def f32(*shape):
    return jax.ShapeDtypeStruct(shape, jnp.float32)


def owner_of():
    return lax.axis_index("grp") * lax.axis_size("row") + lax.axis_index("row")


def dot(a, b, ca, cb):
    return lax.dot_general(
        a, b, (((ca,), (cb,)), ((), ())), precision=HIGHEST, preferred_element_type=jnp.float32
    )


def factor_small(cols):
    n = len(cols)
    d = [[cols[k][i] if i >= k else None for k in range(n)] for i in range(n)]
    low = [[None] * n for _ in range(n)]
    inv = [[None] * n for _ in range(n)]
    for k in range(n):
        root = lax.rsqrt(d[k][k])
        inv[k][k] = root
        for i in range(k + 1, n):
            low[i][k] = d[i][k] * root
        for i in range(k + 1, n):
            for j in range(k + 1, i + 1):
                d[i][j] = d[i][j] - low[i][k] * low[j][k]
        for j in range(k):
            total = low[k][j] * inv[j][j]
            for m in range(j + 1, k):
                total = total + low[k][m] * inv[m][j]
            inv[k][j] = -root * total
    return inv


def factor_block(groups):
    count = len(groups)
    shape = (SUB, BLK)
    sub = lax.broadcasted_iota(jnp.int32, shape, 0)
    lane = lax.broadcasted_iota(jnp.int32, shape, 1)
    spread_row = lambda v, i: jnp.broadcast_to(v[i : i + 1, :], shape)
    spread_col = lambda v, c: jnp.broadcast_to(v[:, c : c + 1], shape)
    upper, inverse = [], []
    groups = list(groups)
    for b in range(count):
        base = SUB * b
        cur = groups[b]
        here = [spread_col(cur, base + k) for k in range(SUB)]
        inv = factor_small([[spread_row(here[k], i) for i in range(SUB)] for k in range(SUB)])
        inv_col = []
        for k in range(SUB):
            col = jnp.where(sub == k, inv[k][k], 0.0)
            for i in range(k + 1, SUB):
                col = jnp.where(sub == i, inv[i][k], col)
            inv_col.append(col)
        done = inv_col[0] * spread_row(cur, 0)
        for k in range(1, SUB):
            done = done + inv_col[k] * spread_row(cur, k)
        upper.append(jnp.where(lane >= base + sub, done, 0.0))
        kept = done
        for k in range(SUB):
            kept = jnp.where(lane == base + k, inv_col[k], kept)
        inverse.append(jnp.where(lane <= base + sub, kept, 0.0))
        if b + 1 == count:
            break
        inside = (lane >= base) & (lane < base + SUB)
        nxt = groups[b + 1]
        after = [spread_col(nxt, base + k) for k in range(SUB)]
        nxt = jnp.where(inside, 0.0, nxt)
        for i in range(SUB):
            low = after[0] * inv[i][0]
            for k in range(1, i + 1):
                low = low + after[k] * inv[i][k]
            nxt = nxt - low * spread_row(kept, i)
        groups[b + 1] = nxt
        if b + 2 < count:
            change = dot(done[:, base + 2 * SUB :], kept, 0, 0)
            for j in range(b + 2, count):
                at = SUB * (j - b - 2)
                groups[j] = jnp.where(inside, 0.0, groups[j]) - change[at : at + SUB]
    return upper, inverse


def factor_half(source, upper_ref, inverse_ref):
    upper, inverse = factor_block([source[SUB * g : SUB * (g + 1)] for g in range(BLK // SUB)])
    for g in range(BLK // SUB):
        at = slice(SUB * g, SUB * (g + 1))
        upper_ref[at, :] = upper[g]
        inverse_ref[at, :] = inverse[g]


def on_root(few):
    return lax.axis_index("col") == 0 if few else lax.axis_index("col") >= 0


def first_half_kernel(few, *refs):
    sources, (upper_ref, inverse_ref, side_ref, next_ref, pivot_ref) = refs[:-5], refs[-5:]

    @pl.when(on_root(few))
    def _():
        if few:
            grp = lax.axis_index("grp")
            tops = PIVOTS // BLK
            place_rows(pivot_ref, sources[0].at[:, :tops], grp)
            place_rows(pivot_ref, sources[1].at[:, :tops], 1 - grp)
        else:
            pivot_ref[...] = sources[0][...]
        factor_half(pivot_ref[:BLK, :BLK], upper_ref, inverse_ref)
        side = dot(inverse_ref[...], pivot_ref[:BLK, BLK:], 1, 0)
        side_ref[...] = side
        next_ref[...] = pivot_ref[BLK:, BLK:] - dot(side, side, 0, 0)


def second_half_kernel(few, first_ref, side_ref, next_ref, upper_ref, inverse_ref, second_ref):
    @pl.when(on_root(few))
    def _():
        factor_half(next_ref[...], upper_ref, second_ref)
        first, second = first_ref[...], second_ref[...]
        inverse_ref[:BLK, :BLK] = first
        inverse_ref[:BLK, BLK:] = jnp.zeros((BLK, BLK), jnp.float32)
        inverse_ref[BLK:, BLK:] = second
        inverse_ref[BLK:, :BLK] = -dot(second, dot(side_ref[...], first, 0, 0), 1, 0)


def split_kernel(map_ref, strip_ref, front_ref, sums_ref, out_ref, inv_ref):
    owners, row_blocks, part, width = sums_ref.shape
    per = width // BLK
    grp, row, col = (lax.axis_index(a) for a in ("grp", "row", "col"))
    n_row, n_col = lax.axis_size("row"), lax.axis_size("col")
    me = grp * n_row + row
    for q in range(map_ref.shape[1]):
        inv_ref[map_ref[grp, q]] = q
    mine = map_ref[grp, row * n_col + col] - col * row_blocks
    for s in range(per):
        at = pl.multiple_of(inv_ref[s] * BLK, BLK)
        lanes = slice(s * BLK, (s + 1) * BLK)
        for k in range(owners):
            piece = strip_ref[part * k : part * (k + 1), pl.ds(at, BLK)]
            for b in range(row_blocks):
                sums_ref[k, b, :, lanes] = jnp.where(mine == b, piece, 0.0)

    @pl.when(me == 0)
    def _():
        for k in range(owners):
            for b in range(row_blocks):
                at = b * BLK + part * k
                sums_ref[k, b] = sums_ref[k, b] + front_ref[at : at + part, :]

    for k in range(owners):
        for s in range(per):
            at = pl.multiple_of(inv_ref[k * per + s] * BLK, BLK)
            out_ref[k, :, s * BLK : (s + 1) * BLK] = strip_ref[:, pl.ds(at, BLK)]


def place_rows(target_ref, pieces_ref, grp):
    row = lax.axis_index("row")
    n_row, blocks, part, _ = pieces_ref.shape
    for b in range(blocks):
        for r in range(n_row):
            at = pl.multiple_of(b * BLK + (grp * n_row + (row ^ r)) * part, SUB)
            target_ref[pl.ds(at, part), :] = pieces_ref[r, b]


def choose(refs, distance, take):
    for ref, here in zip(refs, (distance == 0, distance == 2, distance % 2 == 1)):
        pl.when(here)(functools.partial(take, ref))


def assemble_kernel(map_ref, front_ref, strips_ref, out_ref):
    n_row, n_col = lax.axis_size("row"), lax.axis_size("col")
    col = lax.axis_index("col")
    row_blocks = out_ref.shape[0] // BLK
    out_ref[...] = front_ref[...]
    for i in range(strips_ref.shape[0]):
        local = map_ref[i // n_row, i % n_row * n_col + col] - col * row_blocks
        start = pl.multiple_of(local * BLK, BLK)
        out_ref[pl.ds(start, BLK), :] += strips_ref[i]


def finish_kernel(few, base_ref, near_ref, far_ref, upper_ref, side_ref, upper2_ref, *refs):
    count = 3 if few else 1
    inverses, parts = refs[:count], refs[count : 2 * count]
    out_ref, rows_c_ref, rows_o_ref, inv_ref = refs[-4:]
    rows, width = out_ref.shape
    grp, col = lax.axis_index("grp"), lax.axis_index("col")
    me = owner_of()

    def take_inverse(ref):
        inv_ref[...] = ref[...]

    def take_part(ref):
        half = ref.shape[0] // 2
        place_rows(rows_o_ref, ref.at[:half], grp)
        place_rows(rows_o_ref, ref.at[half:], 1 - grp)

    if few:
        choose(inverses, col, take_inverse)
        choose(parts, (me * width // rows) ^ col, take_part)
        place_rows(rows_c_ref, near_ref, grp)
        place_rows(rows_c_ref, far_ref, 1 - grp)
    else:
        inv_ref[...] = inverses[0][...]
        rows_o_ref[...] = parts[0][...]
        rows_c_ref[...] = near_ref[...]
    inv = inv_ref[...]
    left = dot(rows_c_ref[...], inv, 1, 1)

    @pl.when(me == 0)
    def _():
        out_ref[...] = left

        @pl.when(col == 0)
        def _():
            out_ref[:BLK, :BLK] = upper_ref[...].T
            out_ref[:BLK, BLK:] = jnp.zeros((BLK, BLK), jnp.float32)
            out_ref[BLK:PIVOTS, :BLK] = side_ref[...].T
            out_ref[BLK:PIVOTS, BLK:] = upper2_ref[...].T

    @pl.when(me != 0)
    def _():
        right = dot(rows_o_ref[...], inv, 1, 1)
        out_ref[...] = base_ref[...] - dot(left, right, 1, 1)

        @pl.when(col == 0)
        def _():
            out_ref[:PIVOTS, :] = jnp.zeros((PIVOTS, width), jnp.float32)


def from_root(value, axis, root):
    mine = lax.axis_index(axis) == root
    return lax.psum(jnp.where(mine, value, jnp.zeros_like(value)), axis)


def gather_wide(front, strip, child_map):
    n_row, n_col = lax.axis_size("row"), lax.axis_size("col")
    owners = lax.axis_size(OWNER)
    rows, width = front.shape
    row_blocks = rows // BLK
    blocks = owners * width // BLK
    me = owner_of()
    col = lax.axis_index("col")
    hits = child_map[lax.axis_index("grp")][None, :] == jnp.arange(blocks)[:, None]
    source = jnp.argmax(hits, axis=1)
    taken = jnp.take(strip.reshape(BLK, -1, BLK), source, axis=1)
    taken = jnp.where(jnp.any(hits, axis=1)[None, :, None], taken, 0.0)
    outgoing = taken.reshape(BLK, owners, width).transpose(1, 0, 2)
    incoming = lax.all_to_all(outgoing, OWNER, split_axis=0, concat_axis=0, tiled=True)
    ids = jnp.arange(owners)
    places = child_map[ids // n_row, ids % n_row * n_col + col] - col * row_blocks
    assembled = front.reshape(row_blocks, BLK, width).at[places].add(incoming).reshape(rows, width)
    rows_c = from_root(assembled, OWNER, 0)
    pivot = from_root(rows_c[:PIVOTS], "col", 0)
    part = lax.dynamic_slice_in_dim(rows_c, me * width % rows, width, 0)
    rows_o = jnp.zeros((width, width), jnp.float32)
    for c in range(n_col):
        low = c * rows // width
        sent = from_root(part, "col", c)
        rows_o = jnp.where((me >= low) & (me < low + rows // width), sent, rows_o)
    return assembled, (rows_c, rows_c), [pivot], rows_o


def over_col(value, roots):
    n_col = lax.axis_size("col")
    axes = OWNER + ("col",)
    cross = [(o * n_col + c, o * n_col + (c ^ 2)) for o, c in enumerate(roots)]
    over_x = lax.ppermute(value, axes, cross)
    held = jnp.where(lax.axis_index("col") == jnp.array(roots)[owner_of()], value, over_x)
    other = [(o * n_col + (c ^ e), o * n_col + (c ^ e ^ 1)) for o, c in enumerate(roots) for e in (0, 2)]
    return [value, over_x, lax.ppermute(held, axes, other)], held


def gather_pieces(front, strip, child_map):
    owners = lax.axis_size(OWNER)
    rows, width = front.shape
    row_blocks = rows // BLK
    part = BLK // owners
    sums, strips = pl.pallas_call(
        split_kernel,
        out_shape=[f32(owners, row_blocks, part, width), f32(owners, BLK, width)],
        in_specs=[SMEM, VMEM, VMEM],
        out_specs=[VMEM] * 2,
        scratch_shapes=[pltpu.SMEM((child_map.shape[1],), jnp.int32)],
        compiler_params=PARAMS,
        name="split",
    )(child_map, strip, front)
    mine = jnp.sum(lax.all_to_all(sums, OWNER, split_axis=0, concat_axis=0, tiled=True), axis=0)
    strips, mine = lax.optimization_barrier((strips, mine))
    n_row = lax.axis_size("row")
    others = [lax.ppermute(mine, "row", [(i, i ^ d) for i in range(n_row)]) for d in range(1, n_row)]
    near = jnp.stack([mine] + others)
    strips = lax.all_to_all(strips, OWNER, split_axis=0, concat_axis=0, tiled=True)
    far = lax.ppermute(near, "grp", [(0, 1), (1, 0)])

    return front, (near, far), [near, far], strips


def body(front, child_blocks, child_map):
    owners = lax.axis_size(OWNER)
    rows, width = front.shape
    blocks = owners * width // BLK
    few = lax.axis_size("grp") == 2 and lax.axis_size("row") == 4 and lax.axis_size("col") == 4
    few = few and BLK % (owners * 8) == 0 and child_map.shape[1] == blocks
    gather = gather_pieces if few else gather_wide
    base, panel, pivot, last = gather(front, child_blocks[0], child_map)
    half = f32(BLK, BLK)
    cost = pl.CostEstimate(flops=8_000_000_000, bytes_accessed=1 << 18, transcendentals=0)
    upper, first, side, rest = pl.pallas_call(
        functools.partial(first_half_kernel, few),
        out_shape=[half] * 4,
        in_specs=[VMEM] * len(pivot),
        out_specs=[VMEM] * 4,
        scratch_shapes=[pltpu.VMEM((PIVOTS, PIVOTS), jnp.float32)],
        compiler_params=PARAMS,
        cost_estimate=cost,
        name="pivot_first",
    )(*pivot)
    if few:
        first, near, far = lax.optimization_barrier((first, *panel))
        at = owner_of() * width % rows // BLK
        cut = lambda v: lax.dynamic_slice_in_dim(v, at, width // BLK, 1)
        own_part = jnp.concatenate([cut(near), cut(far)], axis=0)
        parts, _ = over_col(own_part, [o * width // rows for o in range(owners)])
    upper2, inverse = pl.pallas_call(
        functools.partial(second_half_kernel, few),
        out_shape=[half, f32(PIVOTS, PIVOTS)],
        in_specs=[VMEM] * 3,
        out_specs=[VMEM] * 2,
        scratch_shapes=[pltpu.VMEM((BLK, BLK), jnp.float32)],
        compiler_params=PARAMS,
        cost_estimate=cost,
        name="pivot_second",
    )(first, side, rest)
    if few:
        inverses, held = over_col(inverse, [0] * owners)
        strips, _ = lax.optimization_barrier((last, held))
        base = pl.pallas_call(
            assemble_kernel,
            out_shape=f32(rows, width),
            in_specs=[SMEM, VMEM, VMEM],
            out_specs=VMEM,
            compiler_params=PARAMS,
            name="assemble",
        )(child_map, base, strips)
    else:
        inverses, parts = [inverse], [last]
    return pl.pallas_call(
        functools.partial(finish_kernel, few),
        out_shape=f32(rows, width),
        in_specs=[VMEM] * (6 + len(inverses) + len(parts)),
        out_specs=VMEM,
        scratch_shapes=[pltpu.VMEM((n, width), jnp.float32) for n in (rows, width, PIVOTS)],
        compiler_params=PARAMS,
        name="finish",
    )(base, *panel, upper, side, upper2, *inverses, *parts)


def solution(mesh):
    return jax.shard_map(
        body,
        mesh=mesh,
        in_specs=(P("col", ("grp", "row")), P("grp", ("row", "col"), None), P()),
        out_specs=P("col", ("grp", "row")),
        check_vma=False,
    )
```

```python
import functools

import jax
import jax.numpy as jnp
from jax import lax
from jax.experimental import pallas as pl
from jax.experimental.pallas import tpu as pltpu
from jax.sharding import PartitionSpec as P

BLK = 128
PIVOTS = 256
OWNER = ("grp", "row")
HIGHEST = lax.Precision.HIGHEST
SUB = 8
VMEM = pl.BlockSpec(memory_space=pltpu.VMEM)
SMEM = pl.BlockSpec(memory_space=pltpu.SMEM)
PARAMS = pltpu.CompilerParams(vmem_limit_bytes=48 * 1024 * 1024)


def f32(*shape):
    return jax.ShapeDtypeStruct(shape, jnp.float32)


def owner_of():
    return lax.axis_index("grp") * lax.axis_size("row") + lax.axis_index("row")


def dot(a, b, ca, cb):
    return lax.dot_general(
        a, b, (((ca,), (cb,)), ((), ())), precision=HIGHEST, preferred_element_type=jnp.float32
    )


def factor_small(cols):
    n = len(cols)
    d = [[cols[k][i] if i >= k else None for k in range(n)] for i in range(n)]
    low = [[None] * n for _ in range(n)]
    inv = [[None] * n for _ in range(n)]
    for k in range(n):
        root = lax.rsqrt(d[k][k])
        inv[k][k] = root
        for i in range(k + 1, n):
            low[i][k] = d[i][k] * root
        for i in range(k + 1, n):
            for j in range(k + 1, i + 1):
                d[i][j] = d[i][j] - low[i][k] * low[j][k]
        for j in range(k):
            total = low[k][j] * inv[j][j]
            for m in range(j + 1, k):
                total = total + low[k][m] * inv[m][j]
            inv[k][j] = -root * total
    return inv


def factor_block(groups):
    count = len(groups)
    shape = (SUB, BLK)
    sub = lax.broadcasted_iota(jnp.int32, shape, 0)
    lane = lax.broadcasted_iota(jnp.int32, shape, 1)
    spread_row = lambda v, i: jnp.broadcast_to(v[i : i + 1, :], shape)
    spread_col = lambda v, c: jnp.broadcast_to(v[:, c : c + 1], shape)
    upper, inverse = [], []
    groups = list(groups)
    for b in range(count):
        base = SUB * b
        cur = groups[b]
        here = [spread_col(cur, base + k) for k in range(SUB)]
        inv = factor_small([[spread_row(here[k], i) for i in range(SUB)] for k in range(SUB)])
        inv_col = []
        for k in range(SUB):
            col = jnp.where(sub == k, inv[k][k], 0.0)
            for i in range(k + 1, SUB):
                col = jnp.where(sub == i, inv[i][k], col)
            inv_col.append(col)
        done = inv_col[0] * spread_row(cur, 0)
        for k in range(1, SUB):
            done = done + inv_col[k] * spread_row(cur, k)
        upper.append(jnp.where(lane >= base + sub, done, 0.0))
        kept = done
        for k in range(SUB):
            kept = jnp.where(lane == base + k, inv_col[k], kept)
        inverse.append(jnp.where(lane <= base + sub, kept, 0.0))
        if b + 1 == count:
            break
        inside = (lane >= base) & (lane < base + SUB)
        nxt = groups[b + 1]
        after = [spread_col(nxt, base + k) for k in range(SUB)]
        nxt = jnp.where(inside, 0.0, nxt)
        for i in range(SUB):
            low = after[0] * inv[i][0]
            for k in range(1, i + 1):
                low = low + after[k] * inv[i][k]
            nxt = nxt - low * spread_row(kept, i)
        groups[b + 1] = nxt
        if b + 2 < count:
            change = dot(done[:, base + 2 * SUB :], kept, 0, 0)
            for j in range(b + 2, count):
                at = SUB * (j - b - 2)
                groups[j] = jnp.where(inside, 0.0, groups[j]) - change[at : at + SUB]
    return upper, inverse


def factor_half(source, upper_ref, inverse_ref):
    upper, inverse = factor_block([source[SUB * g : SUB * (g + 1)] for g in range(BLK // SUB)])
    for g in range(BLK // SUB):
        at = slice(SUB * g, SUB * (g + 1))
        upper_ref[at, :] = upper[g]
        inverse_ref[at, :] = inverse[g]


def on_root(few):
    return lax.axis_index("col") == 0 if few else lax.axis_index("col") >= 0


def first_half_kernel(few, *refs):
    sources, (upper_ref, inverse_ref, side_ref, next_ref, pivot_ref) = refs[:-5], refs[-5:]

    @pl.when(on_root(few))
    def _():
        if few:
            grp = lax.axis_index("grp")
            tops = PIVOTS // BLK
            place_rows(pivot_ref, sources[0].at[:, :tops], grp)
            place_rows(pivot_ref, sources[1].at[:, :tops], 1 - grp)
        else:
            pivot_ref[...] = sources[0][...]
        factor_half(pivot_ref[:BLK, :BLK], upper_ref, inverse_ref)
        side = dot(inverse_ref[...], pivot_ref[:BLK, BLK:], 1, 0)
        side_ref[...] = side
        next_ref[...] = pivot_ref[BLK:, BLK:] - dot(side, side, 0, 0)


def second_half_kernel(few, first_ref, side_ref, next_ref, upper_ref, inverse_ref, second_ref):
    @pl.when(on_root(few))
    def _():
        factor_half(next_ref[...], upper_ref, second_ref)
        first, second = first_ref[...], second_ref[...]
        inverse_ref[:BLK, :BLK] = first
        inverse_ref[:BLK, BLK:] = jnp.zeros((BLK, BLK), jnp.float32)
        inverse_ref[BLK:, BLK:] = second
        inverse_ref[BLK:, :BLK] = -dot(second, dot(side_ref[...], first, 0, 0), 1, 0)


def split_kernel(map_ref, strip_ref, panel_ref, out_ref, inv_ref):
    owners, part, width = panel_ref.shape
    per = width // BLK
    grp = lax.axis_index("grp")
    for q in range(map_ref.shape[1]):
        inv_ref[map_ref[grp, q]] = q
    for k in range(owners):
        for s in range(per):
            at = pl.multiple_of(inv_ref[k * per + s] * BLK, BLK)
            out_ref[k, :, s * BLK : (s + 1) * BLK] = strip_ref[:, pl.ds(at, BLK)]
    for k in range(owners):
        panel_ref[k] = out_ref[0, part * k : part * (k + 1), :]


def sum_panel_kernel(map_ref, low_ref, high_ref, pieces_ref, out_ref):
    n_row, n_col = lax.axis_size("row"), lax.axis_size("col")
    grp, col = lax.axis_index("grp"), lax.axis_index("col")
    blocks = out_ref.shape[0]
    out_ref[...] = jnp.where(grp == 0, low_ref[...], high_ref[...])
    for i in range(pieces_ref.shape[0]):
        local = map_ref[i // n_row, i % n_row * n_col + col] - col * blocks
        out_ref[local] = out_ref[local] + pieces_ref[i]


def place_rows(target_ref, pieces_ref, grp):
    row = lax.axis_index("row")
    n_row, blocks, part, _ = pieces_ref.shape
    for b in range(blocks):
        for r in range(n_row):
            at = pl.multiple_of(b * BLK + (grp * n_row + (row ^ r)) * part, SUB)
            target_ref[pl.ds(at, part), :] = pieces_ref[r, b]


def choose(refs, distance, take):
    for ref, here in zip(refs, (distance == 0, distance == 2, distance % 2 == 1)):
        pl.when(here)(functools.partial(take, ref))


def assemble_kernel(map_ref, front_ref, strips_ref, out_ref):
    n_row, n_col = lax.axis_size("row"), lax.axis_size("col")
    col = lax.axis_index("col")
    row_blocks = out_ref.shape[0] // BLK
    out_ref[...] = front_ref[...]
    for i in range(strips_ref.shape[0]):
        local = map_ref[i // n_row, i % n_row * n_col + col] - col * row_blocks
        start = pl.multiple_of(local * BLK, BLK)
        out_ref[pl.ds(start, BLK), :] += strips_ref[i]


def finish_kernel(few, base_ref, near_ref, far_ref, upper_ref, side_ref, upper2_ref, *refs):
    count = 3 if few else 1
    inverses, parts = refs[:count], refs[count : 2 * count]
    out_ref, rows_c_ref, rows_o_ref, inv_ref = refs[-4:]
    rows, width = out_ref.shape
    grp, col = lax.axis_index("grp"), lax.axis_index("col")
    me = owner_of()

    def take_inverse(ref):
        inv_ref[...] = ref[...]

    def take_part(ref):
        half = ref.shape[0] // 2
        place_rows(rows_o_ref, ref.at[:half], grp)
        place_rows(rows_o_ref, ref.at[half:], 1 - grp)

    if few:
        choose(inverses, col, take_inverse)
        choose(parts, (me * width // rows) ^ col, take_part)
        place_rows(rows_c_ref, near_ref, grp)
        place_rows(rows_c_ref, far_ref, 1 - grp)
    else:
        inv_ref[...] = inverses[0][...]
        rows_o_ref[...] = parts[0][...]
        rows_c_ref[...] = near_ref[...]
    inv = inv_ref[...]
    left = dot(rows_c_ref[...], inv, 1, 1)

    @pl.when(me == 0)
    def _():
        out_ref[...] = left

        @pl.when(col == 0)
        def _():
            out_ref[:BLK, :BLK] = upper_ref[...].T
            out_ref[:BLK, BLK:] = jnp.zeros((BLK, BLK), jnp.float32)
            out_ref[BLK:PIVOTS, :BLK] = side_ref[...].T
            out_ref[BLK:PIVOTS, BLK:] = upper2_ref[...].T

    @pl.when(me != 0)
    def _():
        right = dot(rows_o_ref[...], inv, 1, 1)
        out_ref[...] = base_ref[...] - dot(left, right, 1, 1)

        @pl.when(col == 0)
        def _():
            out_ref[:PIVOTS, :] = jnp.zeros((PIVOTS, width), jnp.float32)


def from_root(value, axis, root):
    mine = lax.axis_index(axis) == root
    return lax.psum(jnp.where(mine, value, jnp.zeros_like(value)), axis)


def gather_wide(front, strip, child_map):
    n_row, n_col = lax.axis_size("row"), lax.axis_size("col")
    owners = lax.axis_size(OWNER)
    rows, width = front.shape
    row_blocks = rows // BLK
    blocks = owners * width // BLK
    me = owner_of()
    col = lax.axis_index("col")
    hits = child_map[lax.axis_index("grp")][None, :] == jnp.arange(blocks)[:, None]
    source = jnp.argmax(hits, axis=1)
    taken = jnp.take(strip.reshape(BLK, -1, BLK), source, axis=1)
    taken = jnp.where(jnp.any(hits, axis=1)[None, :, None], taken, 0.0)
    outgoing = taken.reshape(BLK, owners, width).transpose(1, 0, 2)
    incoming = lax.all_to_all(outgoing, OWNER, split_axis=0, concat_axis=0, tiled=True)
    ids = jnp.arange(owners)
    places = child_map[ids // n_row, ids % n_row * n_col + col] - col * row_blocks
    assembled = front.reshape(row_blocks, BLK, width).at[places].add(incoming).reshape(rows, width)
    rows_c = from_root(assembled, OWNER, 0)
    pivot = from_root(rows_c[:PIVOTS], "col", 0)
    part = lax.dynamic_slice_in_dim(rows_c, me * width % rows, width, 0)
    rows_o = jnp.zeros((width, width), jnp.float32)
    for c in range(n_col):
        low = c * rows // width
        sent = from_root(part, "col", c)
        rows_o = jnp.where((me >= low) & (me < low + rows // width), sent, rows_o)
    return assembled, (rows_c, rows_c), [pivot], rows_o


def over_col(value, roots):
    n_col = lax.axis_size("col")
    axes = OWNER + ("col",)
    cross = [(o * n_col + c, o * n_col + (c ^ 2)) for o, c in enumerate(roots)]
    over_x = lax.ppermute(value, axes, cross)
    held = jnp.where(lax.axis_index("col") == jnp.array(roots)[owner_of()], value, over_x)
    other = [(o * n_col + (c ^ e), o * n_col + (c ^ e ^ 1)) for o, c in enumerate(roots) for e in (0, 2)]
    return [value, over_x, lax.ppermute(held, axes, other)], held


def gather_pieces(front, strip, child_map):
    owners = lax.axis_size(OWNER)
    rows, width = front.shape
    row_blocks = rows // BLK
    part = BLK // owners
    n_row = lax.axis_size("row")
    cut = front.reshape(row_blocks, owners // n_row, n_row, part, width)
    got = jnp.where(owner_of() == 0, cut[:, :, 0], 0.0)
    for r in range(1, n_row):
        got = got + lax.ppermute(cut[:, :, r], OWNER, [(0, r)])
    low = got[:, 0]
    high = lax.ppermute(got[:, 1], OWNER, [(r, n_row + r) for r in range(n_row)])
    panel, strips = pl.pallas_call(
        split_kernel,
        out_shape=[f32(owners, part, width), f32(owners, BLK, width)],
        in_specs=[SMEM, VMEM],
        out_specs=[VMEM] * 2,
        scratch_shapes=[pltpu.SMEM((child_map.shape[1],), jnp.int32)],
        compiler_params=PARAMS,
        name="split",
    )(child_map, strip)
    pieces = lax.all_to_all(panel, OWNER, split_axis=0, concat_axis=0, tiled=True)
    mine = pl.pallas_call(
        sum_panel_kernel,
        out_shape=f32(row_blocks, part, width),
        in_specs=[SMEM, VMEM, VMEM, VMEM],
        out_specs=VMEM,
        compiler_params=PARAMS,
        name="sum_panel",
    )(child_map, low, high, pieces)
    strips, mine = lax.optimization_barrier((strips, mine))
    others = [lax.ppermute(mine, "row", [(i, i ^ d) for i in range(n_row)]) for d in range(1, n_row)]
    near = jnp.stack([mine] + others)
    strips = lax.all_to_all(strips, OWNER, split_axis=0, concat_axis=0, tiled=True)
    far = lax.ppermute(near, "grp", [(0, 1), (1, 0)])

    return front, (near, far), [near, far], strips


def body(front, child_blocks, child_map):
    owners = lax.axis_size(OWNER)
    rows, width = front.shape
    blocks = owners * width // BLK
    few = lax.axis_size("grp") == 2 and lax.axis_size("row") == 4 and lax.axis_size("col") == 4
    few = few and BLK % (owners * 8) == 0 and child_map.shape[1] == blocks
    gather = gather_pieces if few else gather_wide
    base, panel, pivot, last = gather(front, child_blocks[0], child_map)
    half = f32(BLK, BLK)
    cost = pl.CostEstimate(flops=8_000_000_000, bytes_accessed=1 << 18, transcendentals=0)
    upper, first, side, rest = pl.pallas_call(
        functools.partial(first_half_kernel, few),
        out_shape=[half] * 4,
        in_specs=[VMEM] * len(pivot),
        out_specs=[VMEM] * 4,
        scratch_shapes=[pltpu.VMEM((PIVOTS, PIVOTS), jnp.float32)],
        compiler_params=PARAMS,
        cost_estimate=cost,
        name="pivot_first",
    )(*pivot)
    if few:
        first, near, far = lax.optimization_barrier((first, *panel))
        at = owner_of() * width % rows // BLK
        cut = lambda v: lax.dynamic_slice_in_dim(v, at, width // BLK, 1)
        own_part = jnp.concatenate([cut(near), cut(far)], axis=0)
        parts, _ = over_col(own_part, [o * width // rows for o in range(owners)])
    upper2, inverse = pl.pallas_call(
        functools.partial(second_half_kernel, few),
        out_shape=[half, f32(PIVOTS, PIVOTS)],
        in_specs=[VMEM] * 3,
        out_specs=[VMEM] * 2,
        scratch_shapes=[pltpu.VMEM((BLK, BLK), jnp.float32)],
        compiler_params=PARAMS,
        cost_estimate=cost,
        name="pivot_second",
    )(first, side, rest)
    if few:
        inverses, held = over_col(inverse, [0] * owners)
        strips, _ = lax.optimization_barrier((last, held))
        base = pl.pallas_call(
            assemble_kernel,
            out_shape=f32(rows, width),
            in_specs=[SMEM, VMEM, VMEM],
            out_specs=VMEM,
            compiler_params=PARAMS,
            name="assemble",
        )(child_map, base, strips)
    else:
        inverses, parts = [inverse], [last]
    return pl.pallas_call(
        functools.partial(finish_kernel, few),
        out_shape=f32(rows, width),
        in_specs=[VMEM] * (6 + len(inverses) + len(parts)),
        out_specs=VMEM,
        scratch_shapes=[pltpu.VMEM((n, width), jnp.float32) for n in (rows, width, PIVOTS)],
        compiler_params=PARAMS,
        name="finish",
    )(base, *panel, upper, side, upper2, *inverses, *parts)


def solution(mesh):
    return jax.shard_map(
        body,
        mesh=mesh,
        in_specs=(P("col", ("grp", "row")), P("grp", ("row", "col"), None), P()),
        out_specs=P("col", ("grp", "row")),
        check_vma=False,
    )
```

```python
import functools

import jax
import jax.numpy as jnp
from jax import lax
from jax.experimental import pallas as pl
from jax.experimental.pallas import tpu as pltpu
from jax.sharding import PartitionSpec as P

BLK = 128
PIVOTS = 256
OWNER = ("grp", "row")
HIGHEST = lax.Precision.HIGHEST
SUB = 8
VMEM = pl.BlockSpec(memory_space=pltpu.VMEM)
SMEM = pl.BlockSpec(memory_space=pltpu.SMEM)
PARAMS = pltpu.CompilerParams(vmem_limit_bytes=48 * 1024 * 1024)


def f32(*shape):
    return jax.ShapeDtypeStruct(shape, jnp.float32)


def owner_of():
    return lax.axis_index("grp") * lax.axis_size("row") + lax.axis_index("row")


def dot(a, b, ca, cb):
    return lax.dot_general(
        a, b, (((ca,), (cb,)), ((), ())), precision=HIGHEST, preferred_element_type=jnp.float32
    )


def factor_small(cols):
    n = len(cols)
    d = [[cols[k][i] if i >= k else None for k in range(n)] for i in range(n)]
    low = [[None] * n for _ in range(n)]
    inv = [[None] * n for _ in range(n)]
    for k in range(n):
        root = lax.rsqrt(d[k][k])
        inv[k][k] = root
        for i in range(k + 1, n):
            low[i][k] = d[i][k] * root
        for i in range(k + 1, n):
            for j in range(k + 1, i + 1):
                d[i][j] = d[i][j] - low[i][k] * low[j][k]
        for j in range(k):
            total = low[k][j] * inv[j][j]
            for m in range(j + 1, k):
                total = total + low[k][m] * inv[m][j]
            inv[k][j] = -root * total
    return inv


def factor_block(groups):
    count = len(groups)
    shape = (SUB, BLK)
    sub = lax.broadcasted_iota(jnp.int32, shape, 0)
    lane = lax.broadcasted_iota(jnp.int32, shape, 1)
    spread_row = lambda v, i: jnp.broadcast_to(v[i : i + 1, :], shape)
    spread_col = lambda v, c: jnp.broadcast_to(v[:, c : c + 1], shape)
    upper, inverse = [], []
    groups = list(groups)
    for b in range(count):
        base = SUB * b
        cur = groups[b]
        here = [spread_col(cur, base + k) for k in range(SUB)]
        inv = factor_small([[spread_row(here[k], i) for i in range(SUB)] for k in range(SUB)])
        inv_col = []
        for k in range(SUB):
            col = jnp.where(sub == k, inv[k][k], 0.0)
            for i in range(k + 1, SUB):
                col = jnp.where(sub == i, inv[i][k], col)
            inv_col.append(col)
        done = inv_col[0] * spread_row(cur, 0)
        for k in range(1, SUB):
            done = done + inv_col[k] * spread_row(cur, k)
        upper.append(jnp.where(lane >= base + sub, done, 0.0))
        kept = done
        for k in range(SUB):
            kept = jnp.where(lane == base + k, inv_col[k], kept)
        inverse.append(jnp.where(lane <= base + sub, kept, 0.0))
        if b + 1 == count:
            break
        inside = (lane >= base) & (lane < base + SUB)
        nxt = groups[b + 1]
        after = [spread_col(nxt, base + k) for k in range(SUB)]
        nxt = jnp.where(inside, 0.0, nxt)
        for i in range(SUB):
            low = after[0] * inv[i][0]
            for k in range(1, i + 1):
                low = low + after[k] * inv[i][k]
            nxt = nxt - low * spread_row(kept, i)
        groups[b + 1] = nxt
        if b + 2 < count:
            change = dot(done[:, base + 2 * SUB :], kept, 0, 0)
            for j in range(b + 2, count):
                at = SUB * (j - b - 2)
                groups[j] = jnp.where(inside, 0.0, groups[j]) - change[at : at + SUB]
    return upper, inverse


def factor_half(source, upper_ref, inverse_ref):
    upper, inverse = factor_block([source[SUB * g : SUB * (g + 1)] for g in range(BLK // SUB)])
    for g in range(BLK // SUB):
        at = slice(SUB * g, SUB * (g + 1))
        upper_ref[at, :] = upper[g]
        inverse_ref[at, :] = inverse[g]


def on_root(few):
    return lax.axis_index("col") == 0 if few else lax.axis_index("col") >= 0


def first_half_kernel(few, *refs):
    sources, (upper_ref, inverse_ref, side_ref, next_ref, pivot_ref) = refs[:-5], refs[-5:]

    @pl.when(on_root(few))
    def _():
        if few:
            grp = lax.axis_index("grp")
            tops = PIVOTS // BLK
            place_rows(pivot_ref, sources[0].at[:, :tops], grp)
            place_rows(pivot_ref, sources[1], 1 - grp)
        else:
            pivot_ref[...] = sources[0][...]
        factor_half(pivot_ref[:BLK, :BLK], upper_ref, inverse_ref)
        side = dot(inverse_ref[...], pivot_ref[:BLK, BLK:], 1, 0)
        side_ref[...] = side
        next_ref[...] = pivot_ref[BLK:, BLK:] - dot(side, side, 0, 0)


def second_half_kernel(few, first_ref, side_ref, next_ref, upper_ref, inverse_ref, second_ref):
    @pl.when(on_root(few))
    def _():
        factor_half(next_ref[...], upper_ref, second_ref)
        first, second = first_ref[...], second_ref[...]
        inverse_ref[:BLK, :BLK] = first
        inverse_ref[:BLK, BLK:] = jnp.zeros((BLK, BLK), jnp.float32)
        inverse_ref[BLK:, BLK:] = second
        inverse_ref[BLK:, :BLK] = -dot(second, dot(side_ref[...], first, 0, 0), 1, 0)


def split_kernel(map_ref, strip_ref, panel_ref, out_ref, inv_ref):
    owners, part, width = panel_ref.shape
    per = width // BLK
    grp = lax.axis_index("grp")
    for q in range(map_ref.shape[1]):
        inv_ref[map_ref[grp, q]] = q
    for k in range(owners):
        for s in range(per):
            at = pl.multiple_of(inv_ref[k * per + s] * BLK, BLK)
            out_ref[k, :, s * BLK : (s + 1) * BLK] = strip_ref[:, pl.ds(at, BLK)]
    for k in range(owners):
        panel_ref[k] = out_ref[0, part * k : part * (k + 1), :]


def sum_panel_kernel(map_ref, low_ref, high_ref, pieces_ref, out_ref):
    n_row, n_col = lax.axis_size("row"), lax.axis_size("col")
    grp, col = lax.axis_index("grp"), lax.axis_index("col")
    blocks = out_ref.shape[0]
    out_ref[...] = jnp.where(grp == 0, low_ref[...], high_ref[...])
    for i in range(pieces_ref.shape[0]):
        local = map_ref[i // n_row, i % n_row * n_col + col] - col * blocks
        out_ref[local] = out_ref[local] + pieces_ref[i]


def place_rows(target_ref, pieces_ref, grp, first=0):
    row = lax.axis_index("row")
    n_row, blocks, part, _ = pieces_ref.shape
    for b in range(blocks):
        for r in range(n_row):
            at = pl.multiple_of((first + b) * BLK + (grp * n_row + (row ^ r)) * part, SUB)
            target_ref[pl.ds(at, part), :] = pieces_ref[r, b]


def choose(refs, distance, take):
    for ref, here in zip(refs, (distance == 0, distance == 2, distance % 2 == 1)):
        pl.when(here)(functools.partial(take, ref))


def assemble_kernel(map_ref, front_ref, strips_ref, out_ref):
    n_row, n_col = lax.axis_size("row"), lax.axis_size("col")
    col = lax.axis_index("col")
    row_blocks = out_ref.shape[0] // BLK
    out_ref[...] = front_ref[...]
    for i in range(strips_ref.shape[0]):
        local = map_ref[i // n_row, i % n_row * n_col + col] - col * row_blocks
        start = pl.multiple_of(local * BLK, BLK)
        out_ref[pl.ds(start, BLK), :] += strips_ref[i]


def finish_kernel(few, base_ref, *refs):
    count = 3 if few else 1
    panel, (upper_ref, side_ref, upper2_ref), refs = refs[:count], refs[count : count + 3], refs[count + 3 :]
    inverses, parts = refs[:count], refs[count : 2 * count]
    out_ref, rows_c_ref, rows_o_ref, inv_ref = refs[-4:]
    rows, width = out_ref.shape
    grp, col = lax.axis_index("grp"), lax.axis_index("col")
    me = owner_of()

    def take_inverse(ref):
        inv_ref[...] = ref[...]

    def take_part(ref):
        half = ref.shape[0] // 2
        place_rows(rows_o_ref, ref.at[:half], grp)
        place_rows(rows_o_ref, ref.at[half:], 1 - grp)

    if few:
        choose(inverses, col, take_inverse)
        choose(parts, (me * width // rows) ^ col, take_part)
        near_ref, far_top_ref, far_rest_ref = panel
        place_rows(rows_c_ref, near_ref, grp)
        place_rows(rows_c_ref, far_top_ref, 1 - grp)
        place_rows(rows_c_ref, far_rest_ref, 1 - grp, far_top_ref.shape[1])
    else:
        inv_ref[...] = inverses[0][...]
        rows_o_ref[...] = parts[0][...]
        rows_c_ref[...] = panel[0][...]
    inv = inv_ref[...]
    left = dot(rows_c_ref[...], inv, 1, 1)

    @pl.when(me == 0)
    def _():
        out_ref[...] = left

        @pl.when(col == 0)
        def _():
            out_ref[:BLK, :BLK] = upper_ref[...].T
            out_ref[:BLK, BLK:] = jnp.zeros((BLK, BLK), jnp.float32)
            out_ref[BLK:PIVOTS, :BLK] = side_ref[...].T
            out_ref[BLK:PIVOTS, BLK:] = upper2_ref[...].T

    @pl.when(me != 0)
    def _():
        right = dot(rows_o_ref[...], inv, 1, 1)
        out_ref[...] = base_ref[...] - dot(left, right, 1, 1)

        @pl.when(col == 0)
        def _():
            out_ref[:PIVOTS, :] = jnp.zeros((PIVOTS, width), jnp.float32)


def from_root(value, axis, root):
    mine = lax.axis_index(axis) == root
    return lax.psum(jnp.where(mine, value, jnp.zeros_like(value)), axis)


def gather_wide(front, strip, child_map):
    n_row, n_col = lax.axis_size("row"), lax.axis_size("col")
    owners = lax.axis_size(OWNER)
    rows, width = front.shape
    row_blocks = rows // BLK
    blocks = owners * width // BLK
    me = owner_of()
    col = lax.axis_index("col")
    hits = child_map[lax.axis_index("grp")][None, :] == jnp.arange(blocks)[:, None]
    source = jnp.argmax(hits, axis=1)
    taken = jnp.take(strip.reshape(BLK, -1, BLK), source, axis=1)
    taken = jnp.where(jnp.any(hits, axis=1)[None, :, None], taken, 0.0)
    outgoing = taken.reshape(BLK, owners, width).transpose(1, 0, 2)
    incoming = lax.all_to_all(outgoing, OWNER, split_axis=0, concat_axis=0, tiled=True)
    ids = jnp.arange(owners)
    places = child_map[ids // n_row, ids % n_row * n_col + col] - col * row_blocks
    assembled = front.reshape(row_blocks, BLK, width).at[places].add(incoming).reshape(rows, width)
    rows_c = from_root(assembled, OWNER, 0)
    pivot = from_root(rows_c[:PIVOTS], "col", 0)
    part = lax.dynamic_slice_in_dim(rows_c, me * width % rows, width, 0)
    rows_o = jnp.zeros((width, width), jnp.float32)
    for c in range(n_col):
        low = c * rows // width
        sent = from_root(part, "col", c)
        rows_o = jnp.where((me >= low) & (me < low + rows // width), sent, rows_o)
    return assembled, [rows_c], [pivot], rows_o


def over_col(value, roots, root):
    n_col = lax.axis_size("col")
    axes = OWNER + ("col",)
    cross = [(o * n_col + c, o * n_col + (c ^ 2)) for o, c in enumerate(roots)]
    over_x = lax.ppermute(value, axes, cross)
    held = jnp.where(lax.axis_index("col") == root, value, over_x)
    other = [(o * n_col + (c ^ e), o * n_col + (c ^ e ^ 1)) for o, c in enumerate(roots) for e in (0, 2)]
    return [value, over_x, lax.ppermute(held, axes, other)], held


def gather_pieces(front, strip, child_map):
    owners = lax.axis_size(OWNER)
    rows, width = front.shape
    row_blocks = rows // BLK
    part = BLK // owners
    n_row = lax.axis_size("row")
    cut = front.reshape(row_blocks, owners // n_row, n_row, part, width)
    got = jnp.where(owner_of() == 0, cut[:, :, 0], 0.0)
    for r in range(1, n_row):
        got = got + lax.ppermute(cut[:, :, r], OWNER, [(0, r)])
    low = got[:, 0]
    high = lax.ppermute(got[:, 1], OWNER, [(r, n_row + r) for r in range(n_row)])
    panel, strips = pl.pallas_call(
        split_kernel,
        out_shape=[f32(owners, part, width), f32(owners, BLK, width)],
        in_specs=[SMEM, VMEM],
        out_specs=[VMEM] * 2,
        scratch_shapes=[pltpu.SMEM((child_map.shape[1],), jnp.int32)],
        compiler_params=PARAMS,
        name="split",
    )(child_map, strip)
    pieces = lax.all_to_all(panel, OWNER, split_axis=0, concat_axis=0, tiled=True)
    mine = pl.pallas_call(
        sum_panel_kernel,
        out_shape=f32(row_blocks, part, width),
        in_specs=[SMEM, VMEM, VMEM, VMEM],
        out_specs=VMEM,
        compiler_params=PARAMS,
        name="sum_panel",
    )(child_map, low, high, pieces)
    strips, mine = lax.optimization_barrier((strips, mine))
    others = [lax.ppermute(mine, "row", [(i, i ^ d) for i in range(n_row)]) for d in range(1, n_row)]
    near = jnp.stack([mine] + others)
    strips = lax.all_to_all(strips, OWNER, split_axis=0, concat_axis=0, tiled=True)
    far_top = lax.ppermute(near[:, : PIVOTS // BLK], "grp", [(0, 1), (1, 0)])
    return front, [near], [near, far_top], strips


def body(front, child_blocks, child_map):
    owners = lax.axis_size(OWNER)
    rows, width = front.shape
    blocks = owners * width // BLK
    few = lax.axis_size("grp") == 2 and lax.axis_size("row") == 4 and lax.axis_size("col") == 4
    few = few and BLK % (owners * 8) == 0 and child_map.shape[1] == blocks
    few = few and rows == 2 * width and width == PIVOTS
    gather = gather_pieces if few else gather_wide
    base, panel, pivot, last = gather(front, child_blocks[0], child_map)
    half = f32(BLK, BLK)
    cost = pl.CostEstimate(flops=8_000_000_000, bytes_accessed=1 << 18, transcendentals=0)
    upper, first, side, rest = pl.pallas_call(
        functools.partial(first_half_kernel, few),
        out_shape=[half] * 4,
        in_specs=[VMEM] * len(pivot),
        out_specs=[VMEM] * 4,
        scratch_shapes=[pltpu.VMEM((PIVOTS, PIVOTS), jnp.float32)],
        compiler_params=PARAMS,
        cost_estimate=cost,
        name="pivot_first",
    )(*pivot)
    if few:
        tops = PIVOTS // BLK
        near, far_top = pivot
        first, later = lax.optimization_barrier((first, near[:, tops:]))
        far_rest = lax.ppermute(later, "grp", [(0, 1), (1, 0)])
        panel = [near, far_top, far_rest]
        root = owner_of() * width // rows
        at = owner_of() * width % rows // BLK
        cut_near = lax.dynamic_slice_in_dim(near, at, width // BLK, 1)
        cut_far = jnp.where(at == 0, far_top, far_rest)
        own_part = jnp.concatenate([cut_near, cut_far], axis=0)
        parts, _ = over_col(own_part, [o * width // rows for o in range(owners)], root)
    upper2, inverse = pl.pallas_call(
        functools.partial(second_half_kernel, few),
        out_shape=[half, f32(PIVOTS, PIVOTS)],
        in_specs=[VMEM] * 3,
        out_specs=[VMEM] * 2,
        scratch_shapes=[pltpu.VMEM((BLK, BLK), jnp.float32)],
        compiler_params=PARAMS,
        cost_estimate=cost,
        name="pivot_second",
    )(first, side, rest)
    if few:
        inverses, held = over_col(inverse, [0] * owners, 0)
        strips, _ = lax.optimization_barrier((last, held))
        base = pl.pallas_call(
            assemble_kernel,
            out_shape=f32(rows, width),
            in_specs=[SMEM, VMEM, VMEM],
            out_specs=VMEM,
            compiler_params=PARAMS,
            name="assemble",
        )(child_map, base, strips)
    else:
        inverses, parts = [inverse], [last]
    return pl.pallas_call(
        functools.partial(finish_kernel, few),
        out_shape=f32(rows, width),
        in_specs=[VMEM] * (4 + len(panel) + len(inverses) + len(parts)),
        out_specs=VMEM,
        scratch_shapes=[pltpu.VMEM((n, width), jnp.float32) for n in (rows, width, PIVOTS)],
        compiler_params=PARAMS,
        name="finish",
    )(base, *panel, upper, side, upper2, *inverses, *parts)


def solution(mesh):
    return jax.shard_map(
        body,
        mesh=mesh,
        in_specs=(P("col", ("grp", "row")), P("grp", ("row", "col"), None), P()),
        out_specs=P("col", ("grp", "row")),
        check_vma=False,
    )
```

```python
import functools

import jax
import jax.numpy as jnp
from jax import lax
from jax.experimental import pallas as pl
from jax.experimental.pallas import tpu as pltpu
from jax.sharding import PartitionSpec as P

BLK = 128
PIVOTS = 256
OWNER = ("grp", "row")
HIGHEST = lax.Precision.HIGHEST
SUB = 8
VMEM = pl.BlockSpec(memory_space=pltpu.VMEM)
SMEM = pl.BlockSpec(memory_space=pltpu.SMEM)
PARAMS = pltpu.CompilerParams(vmem_limit_bytes=48 * 1024 * 1024)


def f32(*shape):
    return jax.ShapeDtypeStruct(shape, jnp.float32)


def owner_of():
    return lax.axis_index("grp") * lax.axis_size("row") + lax.axis_index("row")


def dot(a, b, ca, cb):
    return lax.dot_general(
        a, b, (((ca,), (cb,)), ((), ())), precision=HIGHEST, preferred_element_type=jnp.float32
    )


def factor_small(cols):
    n = len(cols)
    d = [[cols[k][i] if i >= k else None for k in range(n)] for i in range(n)]
    low = [[None] * n for _ in range(n)]
    inv = [[None] * n for _ in range(n)]
    for k in range(n):
        root = lax.rsqrt(d[k][k])
        inv[k][k] = root
        for i in range(k + 1, n):
            low[i][k] = d[i][k] * root
        for i in range(k + 1, n):
            for j in range(k + 1, i + 1):
                d[i][j] = d[i][j] - low[i][k] * low[j][k]
        for j in range(k):
            total = low[k][j] * inv[j][j]
            for m in range(j + 1, k):
                total = total + low[k][m] * inv[m][j]
            inv[k][j] = -root * total
    return inv


def factor_block(groups):
    count = len(groups)
    shape = (SUB, BLK)
    sub = lax.broadcasted_iota(jnp.int32, shape, 0)
    lane = lax.broadcasted_iota(jnp.int32, shape, 1)
    spread_row = lambda v, i: jnp.broadcast_to(v[i : i + 1, :], shape)
    spread_col = lambda v, c: jnp.broadcast_to(v[:, c : c + 1], shape)
    upper, inverse = [], []
    groups = list(groups)
    for b in range(count):
        base = SUB * b
        cur = groups[b]
        here = [spread_col(cur, base + k) for k in range(SUB)]
        inv = factor_small([[spread_row(here[k], i) for i in range(SUB)] for k in range(SUB)])
        inv_col = []
        for k in range(SUB):
            col = jnp.where(sub == k, inv[k][k], 0.0)
            for i in range(k + 1, SUB):
                col = jnp.where(sub == i, inv[i][k], col)
            inv_col.append(col)
        done = inv_col[0] * spread_row(cur, 0)
        for k in range(1, SUB):
            done = done + inv_col[k] * spread_row(cur, k)
        upper.append(jnp.where(lane >= base + sub, done, 0.0))
        kept = done
        for k in range(SUB):
            kept = jnp.where(lane == base + k, inv_col[k], kept)
        inverse.append(jnp.where(lane <= base + sub, kept, 0.0))
        if b + 1 == count:
            break
        inside = (lane >= base) & (lane < base + SUB)
        for j in range(b + 1, min(b + 3, count)):
            nxt = groups[j]
            after = [spread_col(nxt, base + k) for k in range(SUB)]
            nxt = jnp.where(inside, 0.0, nxt)
            for i in range(SUB):
                low = after[0] * inv[i][0]
                for k in range(1, i + 1):
                    low = low + after[k] * inv[i][k]
                nxt = nxt - low * spread_row(kept, i)
            groups[j] = nxt
        if b + 3 < count:
            change = dot(done, kept, 0, 0)
            for j in range(b + 3, count):
                groups[j] = jnp.where(inside, 0.0, groups[j]) - change[SUB * j : SUB * (j + 1)]
    return upper, inverse


def factor_half(source, upper_ref, inverse_ref):
    upper, inverse = factor_block([source[SUB * g : SUB * (g + 1)] for g in range(BLK // SUB)])
    for g in range(BLK // SUB):
        at = slice(SUB * g, SUB * (g + 1))
        upper_ref[at, :] = upper[g]
        inverse_ref[at, :] = inverse[g]


def on_root(few):
    return lax.axis_index("col") == 0 if few else lax.axis_index("col") >= 0


def first_half_kernel(few, *refs):
    sources, (upper_ref, inverse_ref, side_ref, next_ref, pivot_ref) = refs[:-5], refs[-5:]

    @pl.when(on_root(few))
    def _():
        if few:
            grp = lax.axis_index("grp")
            tops = PIVOTS // BLK
            place_rows(pivot_ref, sources[0].at[:, :tops], grp)
            place_rows(pivot_ref, sources[1], 1 - grp)
        else:
            pivot_ref[...] = sources[0][...]
        factor_half(pivot_ref[:BLK, :BLK], upper_ref, inverse_ref)
        side = dot(inverse_ref[...], pivot_ref[:BLK, BLK:], 1, 0)
        side_ref[...] = side
        next_ref[...] = pivot_ref[BLK:, BLK:] - dot(side, side, 0, 0)


def second_half_kernel(few, first_ref, side_ref, next_ref, upper_ref, inverse_ref, second_ref):
    @pl.when(on_root(few))
    def _():
        factor_half(next_ref[...], upper_ref, second_ref)
        first, second = first_ref[...], second_ref[...]
        inverse_ref[:BLK, :BLK] = first
        inverse_ref[:BLK, BLK:] = jnp.zeros((BLK, BLK), jnp.float32)
        inverse_ref[BLK:, BLK:] = second
        inverse_ref[BLK:, :BLK] = -dot(second, dot(side_ref[...], first, 0, 0), 1, 0)


def split_kernel(map_ref, strip_ref, panel_ref, out_ref, inv_ref):
    owners, part, width = panel_ref.shape
    per = width // BLK
    grp = lax.axis_index("grp")
    for q in range(map_ref.shape[1]):
        inv_ref[map_ref[grp, q]] = q
    for k in range(owners):
        for s in range(per):
            at = pl.multiple_of(inv_ref[k * per + s] * BLK, BLK)
            out_ref[k, :, s * BLK : (s + 1) * BLK] = strip_ref[:, pl.ds(at, BLK)]
    for k in range(owners):
        panel_ref[k] = out_ref[0, part * k : part * (k + 1), :]


def sum_panel_kernel(map_ref, low_ref, high_ref, pieces_ref, out_ref):
    n_row, n_col = lax.axis_size("row"), lax.axis_size("col")
    grp, col = lax.axis_index("grp"), lax.axis_index("col")
    blocks = out_ref.shape[0]
    out_ref[...] = jnp.where(grp == 0, low_ref[...], high_ref[...])
    for i in range(pieces_ref.shape[0]):
        local = map_ref[i // n_row, i % n_row * n_col + col] - col * blocks
        out_ref[local] = out_ref[local] + pieces_ref[i]


def place_rows(target_ref, pieces_ref, grp, first=0):
    row = lax.axis_index("row")
    n_row, blocks, part, _ = pieces_ref.shape
    for b in range(blocks):
        for r in range(n_row):
            at = pl.multiple_of((first + b) * BLK + (grp * n_row + (row ^ r)) * part, SUB)
            target_ref[pl.ds(at, part), :] = pieces_ref[r, b]


def choose(refs, distance, take):
    for e, ref in enumerate(refs):
        pl.when(distance == e)(functools.partial(take, ref))


def assemble_kernel(map_ref, front_ref, strips_ref, out_ref):
    n_row, n_col = lax.axis_size("row"), lax.axis_size("col")
    col = lax.axis_index("col")
    row_blocks = out_ref.shape[0] // BLK
    out_ref[...] = front_ref[...]
    for i in range(strips_ref.shape[0]):
        local = map_ref[i // n_row, i % n_row * n_col + col] - col * row_blocks
        start = pl.multiple_of(local * BLK, BLK)
        out_ref[pl.ds(start, BLK), :] += strips_ref[i]


def finish_kernel(few, base_ref, *refs):
    count = 3 if few else 1
    panel, (upper_ref, side_ref, upper2_ref), refs = refs[:count], refs[count : count + 3], refs[count + 3 :]
    count = lax.axis_size("col") if few else 1
    inverses, parts = refs[:count], refs[count : 2 * count]
    out_ref, rows_c_ref, rows_o_ref, inv_ref = refs[-4:]
    rows, width = out_ref.shape
    grp, col = lax.axis_index("grp"), lax.axis_index("col")
    me = owner_of()

    def take_inverse(ref):
        inv_ref[...] = ref[...]

    def take_part(ref):
        half = ref.shape[0] // 2
        place_rows(rows_o_ref, ref.at[:half], grp)
        place_rows(rows_o_ref, ref.at[half:], 1 - grp)

    if few:
        choose(inverses, col, take_inverse)
        choose(parts, (me * width // rows) ^ col, take_part)
        near_ref, far_top_ref, far_rest_ref = panel
        place_rows(rows_c_ref, near_ref, grp)
        place_rows(rows_c_ref, far_top_ref, 1 - grp)
        place_rows(rows_c_ref, far_rest_ref, 1 - grp, far_top_ref.shape[1])
    else:
        inv_ref[...] = inverses[0][...]
        rows_o_ref[...] = parts[0][...]
        rows_c_ref[...] = panel[0][...]
    inv = inv_ref[...]
    left = dot(rows_c_ref[...], inv, 1, 1)

    @pl.when(me == 0)
    def _():
        out_ref[...] = left

        @pl.when(col == 0)
        def _():
            out_ref[:BLK, :BLK] = upper_ref[...].T
            out_ref[:BLK, BLK:] = jnp.zeros((BLK, BLK), jnp.float32)
            out_ref[BLK:PIVOTS, :BLK] = side_ref[...].T
            out_ref[BLK:PIVOTS, BLK:] = upper2_ref[...].T

    @pl.when(me != 0)
    def _():
        right = dot(rows_o_ref[...], inv, 1, 1)
        out_ref[...] = base_ref[...] - dot(left, right, 1, 1)

        @pl.when(col == 0)
        def _():
            out_ref[:PIVOTS, :] = jnp.zeros((PIVOTS, width), jnp.float32)


def from_root(value, axis, root):
    mine = lax.axis_index(axis) == root
    return lax.psum(jnp.where(mine, value, jnp.zeros_like(value)), axis)


def gather_wide(front, strip, child_map):
    n_row, n_col = lax.axis_size("row"), lax.axis_size("col")
    owners = lax.axis_size(OWNER)
    rows, width = front.shape
    row_blocks = rows // BLK
    blocks = owners * width // BLK
    me = owner_of()
    col = lax.axis_index("col")
    hits = child_map[lax.axis_index("grp")][None, :] == jnp.arange(blocks)[:, None]
    source = jnp.argmax(hits, axis=1)
    taken = jnp.take(strip.reshape(BLK, -1, BLK), source, axis=1)
    taken = jnp.where(jnp.any(hits, axis=1)[None, :, None], taken, 0.0)
    outgoing = taken.reshape(BLK, owners, width).transpose(1, 0, 2)
    incoming = lax.all_to_all(outgoing, OWNER, split_axis=0, concat_axis=0, tiled=True)
    ids = jnp.arange(owners)
    places = child_map[ids // n_row, ids % n_row * n_col + col] - col * row_blocks
    assembled = front.reshape(row_blocks, BLK, width).at[places].add(incoming).reshape(rows, width)
    rows_c = from_root(assembled, OWNER, 0)
    pivot = from_root(rows_c[:PIVOTS], "col", 0)
    part = lax.dynamic_slice_in_dim(rows_c, me * width % rows, width, 0)
    rows_o = jnp.zeros((width, width), jnp.float32)
    for c in range(n_col):
        low = c * rows // width
        sent = from_root(part, "col", c)
        rows_o = jnp.where((me >= low) & (me < low + rows // width), sent, rows_o)
    return assembled, [rows_c], [pivot], rows_o


def over_col(value, roots):
    n_col = lax.axis_size("col")
    axes = OWNER + ("col",)
    pairs = lambda e, f: [(o * n_col + (c ^ e), o * n_col + (c ^ f)) for o, c in enumerate(roots)]
    over_x = lax.ppermute(value, axes, pairs(0, 2))
    beside = lax.ppermute(value, axes, pairs(0, 1))
    return [value, beside, over_x, lax.ppermute(over_x, axes, pairs(2, 3))], over_x


def gather_pieces(front, strip, child_map):
    owners = lax.axis_size(OWNER)
    rows, width = front.shape
    row_blocks = rows // BLK
    part = BLK // owners
    n_row = lax.axis_size("row")
    cut = front.reshape(row_blocks, owners // n_row, n_row, part, width)
    got = jnp.where(owner_of() == 0, cut[:, :, 0], 0.0)
    for r in range(1, n_row):
        got = got + lax.ppermute(cut[:, :, r], OWNER, [(0, r)])
    low = got[:, 0]
    high = lax.ppermute(got[:, 1], OWNER, [(r, n_row + r) for r in range(n_row)])
    panel, strips = pl.pallas_call(
        split_kernel,
        out_shape=[f32(owners, part, width), f32(owners, BLK, width)],
        in_specs=[SMEM, VMEM],
        out_specs=[VMEM] * 2,
        scratch_shapes=[pltpu.SMEM((child_map.shape[1],), jnp.int32)],
        compiler_params=PARAMS,
        name="split",
    )(child_map, strip)
    pieces = lax.all_to_all(panel, OWNER, split_axis=0, concat_axis=0, tiled=True)
    mine = pl.pallas_call(
        sum_panel_kernel,
        out_shape=f32(row_blocks, part, width),
        in_specs=[SMEM, VMEM, VMEM, VMEM],
        out_specs=VMEM,
        compiler_params=PARAMS,
        name="sum_panel",
    )(child_map, low, high, pieces)
    strips, mine = lax.optimization_barrier((strips, mine))
    others = [lax.ppermute(mine, "row", [(i, i ^ d) for i in range(n_row)]) for d in range(1, n_row)]
    near = jnp.stack([mine] + others)
    strips = lax.all_to_all(strips, OWNER, split_axis=0, concat_axis=0, tiled=True)
    far_top = lax.ppermute(near[:, : PIVOTS // BLK], "grp", [(0, 1), (1, 0)])
    return front, [near], [near, far_top], strips


def body(front, child_blocks, child_map):
    owners = lax.axis_size(OWNER)
    rows, width = front.shape
    blocks = owners * width // BLK
    few = lax.axis_size("grp") == 2 and lax.axis_size("row") == 4 and lax.axis_size("col") == 4
    few = few and BLK % (owners * 8) == 0 and child_map.shape[1] == blocks
    few = few and rows == 2 * width and width == PIVOTS
    gather = gather_pieces if few else gather_wide
    base, panel, pivot, last = gather(front, child_blocks[0], child_map)
    half = f32(BLK, BLK)
    cost = pl.CostEstimate(flops=8_000_000_000, bytes_accessed=1 << 18, transcendentals=0)
    upper, first, side, rest = pl.pallas_call(
        functools.partial(first_half_kernel, few),
        out_shape=[half] * 4,
        in_specs=[VMEM] * len(pivot),
        out_specs=[VMEM] * 4,
        scratch_shapes=[pltpu.VMEM((PIVOTS, PIVOTS), jnp.float32)],
        compiler_params=PARAMS,
        cost_estimate=cost,
        name="pivot_first",
    )(*pivot)
    if few:
        tops = PIVOTS // BLK
        near, far_top = pivot
        first, later = lax.optimization_barrier((first, near[:, tops:]))
        far_rest = lax.ppermute(later, "grp", [(0, 1), (1, 0)])
        panel = [near, far_top, far_rest]
        at = owner_of() * width % rows // BLK
        cut_near = lax.dynamic_slice_in_dim(near, at, width // BLK, 1)
        cut_far = jnp.where(at == 0, far_top, far_rest)
        own_part = jnp.concatenate([cut_near, cut_far], axis=0)
        parts, _ = over_col(own_part, [o * width // rows for o in range(owners)])
    upper2, inverse = pl.pallas_call(
        functools.partial(second_half_kernel, few),
        out_shape=[half, f32(PIVOTS, PIVOTS)],
        in_specs=[VMEM] * 3,
        out_specs=[VMEM] * 2,
        scratch_shapes=[pltpu.VMEM((BLK, BLK), jnp.float32)],
        compiler_params=PARAMS,
        cost_estimate=cost,
        name="pivot_second",
    )(first, side, rest)
    if few:
        inverses, held = over_col(inverse, [0] * owners)
        strips, _ = lax.optimization_barrier((last, held))
        base = pl.pallas_call(
            assemble_kernel,
            out_shape=f32(rows, width),
            in_specs=[SMEM, VMEM, VMEM],
            out_specs=VMEM,
            compiler_params=PARAMS,
            name="assemble",
        )(child_map, base, strips)
    else:
        inverses, parts = [inverse], [last]
    return pl.pallas_call(
        functools.partial(finish_kernel, few),
        out_shape=f32(rows, width),
        in_specs=[VMEM] * (4 + len(panel) + len(inverses) + len(parts)),
        out_specs=VMEM,
        scratch_shapes=[pltpu.VMEM((n, width), jnp.float32) for n in (rows, width, PIVOTS)],
        compiler_params=PARAMS,
        name="finish",
    )(base, *panel, upper, side, upper2, *inverses, *parts)


def solution(mesh):
    return jax.shard_map(
        body,
        mesh=mesh,
        in_specs=(P("col", ("grp", "row")), P("grp", ("row", "col"), None), P()),
        out_specs=P("col", ("grp", "row")),
        check_vma=False,
    )
```

```python
import functools

import jax
import jax.numpy as jnp
from jax import lax
from jax.experimental import pallas as pl
from jax.experimental.pallas import tpu as pltpu
from jax.sharding import PartitionSpec as P

BLK = 128
PIVOTS = 256
OWNER = ("grp", "row")
HIGHEST = lax.Precision.HIGHEST
SUB = 8
VMEM = pl.BlockSpec(memory_space=pltpu.VMEM)
SMEM = pl.BlockSpec(memory_space=pltpu.SMEM)
PARAMS = pltpu.CompilerParams(vmem_limit_bytes=48 * 1024 * 1024)


def f32(*shape):
    return jax.ShapeDtypeStruct(shape, jnp.float32)


def owner_of():
    return lax.axis_index("grp") * lax.axis_size("row") + lax.axis_index("row")


def dot(a, b, ca, cb):
    return lax.dot_general(
        a, b, (((ca,), (cb,)), ((), ())), precision=HIGHEST, preferred_element_type=jnp.float32
    )


def factor_small(cols):
    n = len(cols)
    d = [[cols[k][i] if i >= k else None for k in range(n)] for i in range(n)]
    low = [[None] * n for _ in range(n)]
    inv = [[None] * n for _ in range(n)]
    for k in range(n):
        root = lax.rsqrt(d[k][k])
        inv[k][k] = root
        for i in range(k + 1, n):
            low[i][k] = d[i][k] * root
        for i in range(k + 1, n):
            for j in range(k + 1, i + 1):
                d[i][j] = d[i][j] - low[i][k] * low[j][k]
        for j in range(k):
            total = low[k][j] * inv[j][j]
            for m in range(j + 1, k):
                total = total + low[k][m] * inv[m][j]
            inv[k][j] = -root * total
    return inv


def factor_block(groups):
    count = len(groups)
    shape = (SUB, BLK)
    sub = lax.broadcasted_iota(jnp.int32, shape, 0)
    lane = lax.broadcasted_iota(jnp.int32, shape, 1)
    spread_row = lambda v, i: jnp.broadcast_to(v[i : i + 1, :], shape)
    spread_col = lambda v, c: jnp.broadcast_to(v[:, c : c + 1], shape)
    upper, inverse = [], []
    groups = list(groups)
    for b in range(count):
        base = SUB * b
        cur = groups[b]
        here = [spread_col(cur, base + k) for k in range(SUB)]
        inv = factor_small([[spread_row(here[k], i) for i in range(SUB)] for k in range(SUB)])
        inv_col = []
        for k in range(SUB):
            col = jnp.where(sub == k, inv[k][k], 0.0)
            for i in range(k + 1, SUB):
                col = jnp.where(sub == i, inv[i][k], col)
            inv_col.append(col)
        done = inv_col[0] * spread_row(cur, 0)
        for k in range(1, SUB):
            done = done + inv_col[k] * spread_row(cur, k)
        upper.append(jnp.where(lane >= base + sub, done, 0.0))
        kept = done
        for k in range(SUB):
            kept = jnp.where(lane == base + k, inv_col[k], kept)
        inverse.append(jnp.where(lane <= base + sub, kept, 0.0))
        if b + 1 == count:
            break
        inside = (lane >= base) & (lane < base + SUB)
        for j in range(b + 1, min(b + 3, count)):
            nxt = groups[j]
            after = [spread_col(nxt, base + k) for k in range(SUB)]
            nxt = jnp.where(inside, 0.0, nxt)
            for i in range(SUB):
                low = after[0] * inv[i][0]
                for k in range(1, i + 1):
                    low = low + after[k] * inv[i][k]
                nxt = nxt - low * spread_row(kept, i)
            groups[j] = nxt
        if b + 3 < count:
            change = dot(done, kept, 0, 0)
            for j in range(b + 3, count):
                groups[j] = jnp.where(inside, 0.0, groups[j]) - change[SUB * j : SUB * (j + 1)]
    return upper, inverse


def factor_half(source, upper_ref, inverse_ref):
    upper, inverse = factor_block([source[SUB * g : SUB * (g + 1)] for g in range(BLK // SUB)])
    for g in range(BLK // SUB):
        at = slice(SUB * g, SUB * (g + 1))
        upper_ref[at, :] = upper[g]
        inverse_ref[at, :] = inverse[g]


def on_root(few):
    return lax.axis_index("col") == 0 if few else lax.axis_index("col") >= 0


def first_half_kernel(few, *refs):
    sources, (upper_ref, inverse_ref, side_ref, next_ref, pivot_ref) = refs[:-5], refs[-5:]

    @pl.when(on_root(few))
    def _():
        if few:
            grp = lax.axis_index("grp")
            tops = PIVOTS // BLK
            place_rows(pivot_ref, sources[0].at[:, :tops], grp)
            place_rows(pivot_ref, sources[1], 1 - grp)
        else:
            pivot_ref[...] = sources[0][...]
        factor_half(pivot_ref[:BLK, :BLK], upper_ref, inverse_ref)
        side = dot(inverse_ref[...], pivot_ref[:BLK, BLK:], 1, 0)
        side_ref[...] = side
        next_ref[...] = pivot_ref[BLK:, BLK:] - dot(side, side, 0, 0)


def second_half_kernel(few, first_ref, side_ref, next_ref, upper_ref, inverse_ref, second_ref):
    @pl.when(on_root(few))
    def _():
        factor_half(next_ref[...], upper_ref, second_ref)
        first, second = first_ref[...], second_ref[...]
        inverse_ref[:BLK, :BLK] = first
        inverse_ref[:BLK, BLK:] = jnp.zeros((BLK, BLK), jnp.float32)
        inverse_ref[BLK:, BLK:] = second
        inverse_ref[BLK:, :BLK] = -dot(second, dot(side_ref[...], first, 0, 0), 1, 0)


def split_kernel(map_ref, strip_ref, panel_ref, out_ref, inv_ref):
    owners, part, width = panel_ref.shape
    per = width // BLK
    grp = lax.axis_index("grp")
    for q in range(map_ref.shape[1]):
        inv_ref[map_ref[grp, q]] = q
    for k in range(owners):
        for s in range(per):
            at = pl.multiple_of(inv_ref[k * per + s] * BLK, BLK)
            out_ref[k, :, s * BLK : (s + 1) * BLK] = strip_ref[:, pl.ds(at, BLK)]
    for k in range(owners):
        panel_ref[k] = out_ref[0, part * k : part * (k + 1), :]


def sum_panel_kernel(map_ref, low_ref, high_ref, pieces_ref, out_ref):
    n_row, n_col = lax.axis_size("row"), lax.axis_size("col")
    grp, col = lax.axis_index("grp"), lax.axis_index("col")
    blocks = out_ref.shape[0]
    out_ref[...] = jnp.where(grp == 0, low_ref[...], high_ref[...])
    for i in range(pieces_ref.shape[0]):
        local = map_ref[i // n_row, i % n_row * n_col + col] - col * blocks
        out_ref[local] = out_ref[local] + pieces_ref[i]


def place_rows(target_ref, pieces_ref, grp, first=0):
    row = lax.axis_index("row")
    n_row, blocks, part, _ = pieces_ref.shape
    for b in range(blocks):
        for r in range(n_row):
            at = pl.multiple_of((first + b) * BLK + (grp * n_row + (row ^ r)) * part, SUB)
            target_ref[pl.ds(at, part), :] = pieces_ref[r, b]


def choose(refs, distance, take):
    for e, ref in enumerate(refs):
        pl.when(distance == e)(functools.partial(take, ref))


def assemble_kernel(map_ref, updated_ref, strips_ref, out_ref):
    n_row, n_col = lax.axis_size("row"), lax.axis_size("col")
    col = lax.axis_index("col")
    row_blocks = out_ref.shape[0] // BLK
    out_ref[...] = updated_ref[...]

    @pl.when(owner_of() != 0)
    def _():
        for i in range(strips_ref.shape[0]):
            local = map_ref[i // n_row, i % n_row * n_col + col] - col * row_blocks
            start = pl.multiple_of(local * BLK, BLK)
            out_ref[pl.ds(start, BLK), :] += strips_ref[i]

        @pl.when(col == 0)
        def _():
            out_ref[:PIVOTS, :] = jnp.zeros((PIVOTS, out_ref.shape[1]), jnp.float32)


def finish_kernel(few, base_ref, *refs):
    count = 3 if few else 1
    panel, (upper_ref, side_ref, upper2_ref), refs = refs[:count], refs[count : count + 3], refs[count + 3 :]
    count = lax.axis_size("col") if few else 1
    inverses, parts = refs[:count], refs[count : 2 * count]
    out_ref, rows_c_ref, rows_o_ref, inv_ref = refs[-4:]
    rows, width = out_ref.shape
    grp, col = lax.axis_index("grp"), lax.axis_index("col")
    me = owner_of()

    def take_inverse(ref):
        inv_ref[...] = ref[...]

    def take_part(ref):
        half = ref.shape[0] // 2
        place_rows(rows_o_ref, ref.at[:half], grp)
        place_rows(rows_o_ref, ref.at[half:], 1 - grp)

    if few:
        choose(inverses, col, take_inverse)
        choose(parts, (me * width // rows) ^ col, take_part)
        near_ref, far_top_ref, far_rest_ref = panel
        place_rows(rows_c_ref, near_ref, grp)
        place_rows(rows_c_ref, far_top_ref, 1 - grp)
        place_rows(rows_c_ref, far_rest_ref, 1 - grp, far_top_ref.shape[1])
    else:
        inv_ref[...] = inverses[0][...]
        rows_o_ref[...] = parts[0][...]
        rows_c_ref[...] = panel[0][...]
    inv = inv_ref[...]
    left = dot(rows_c_ref[...], inv, 1, 1)

    @pl.when(me == 0)
    def _():
        out_ref[...] = left

        @pl.when(col == 0)
        def _():
            out_ref[:BLK, :BLK] = upper_ref[...].T
            out_ref[:BLK, BLK:] = jnp.zeros((BLK, BLK), jnp.float32)
            out_ref[BLK:PIVOTS, :BLK] = side_ref[...].T
            out_ref[BLK:PIVOTS, BLK:] = upper2_ref[...].T

    @pl.when(me != 0)
    def _():
        right = dot(rows_o_ref[...], inv, 1, 1)
        out_ref[...] = base_ref[...] - dot(left, right, 1, 1)

        @pl.when(col == 0)
        def _():
            out_ref[:PIVOTS, :] = jnp.zeros((PIVOTS, width), jnp.float32)


def from_root(value, axis, root):
    mine = lax.axis_index(axis) == root
    return lax.psum(jnp.where(mine, value, jnp.zeros_like(value)), axis)


def gather_wide(front, strip, child_map):
    n_row, n_col = lax.axis_size("row"), lax.axis_size("col")
    owners = lax.axis_size(OWNER)
    rows, width = front.shape
    row_blocks = rows // BLK
    blocks = owners * width // BLK
    me = owner_of()
    col = lax.axis_index("col")
    hits = child_map[lax.axis_index("grp")][None, :] == jnp.arange(blocks)[:, None]
    source = jnp.argmax(hits, axis=1)
    taken = jnp.take(strip.reshape(BLK, -1, BLK), source, axis=1)
    taken = jnp.where(jnp.any(hits, axis=1)[None, :, None], taken, 0.0)
    outgoing = taken.reshape(BLK, owners, width).transpose(1, 0, 2)
    incoming = lax.all_to_all(outgoing, OWNER, split_axis=0, concat_axis=0, tiled=True)
    ids = jnp.arange(owners)
    places = child_map[ids // n_row, ids % n_row * n_col + col] - col * row_blocks
    assembled = front.reshape(row_blocks, BLK, width).at[places].add(incoming).reshape(rows, width)
    rows_c = from_root(assembled, OWNER, 0)
    pivot = from_root(rows_c[:PIVOTS], "col", 0)
    part = lax.dynamic_slice_in_dim(rows_c, me * width % rows, width, 0)
    rows_o = jnp.zeros((width, width), jnp.float32)
    for c in range(n_col):
        low = c * rows // width
        sent = from_root(part, "col", c)
        rows_o = jnp.where((me >= low) & (me < low + rows // width), sent, rows_o)
    return assembled, [rows_c], [pivot], rows_o


def over_col(value, roots):
    n_col = lax.axis_size("col")
    axes = OWNER + ("col",)
    pairs = lambda e, f: [(o * n_col + (c ^ e), o * n_col + (c ^ f)) for o, c in enumerate(roots)]
    over_x = lax.ppermute(value, axes, pairs(0, 2))
    beside = lax.ppermute(value, axes, pairs(0, 1))
    return [value, beside, over_x, lax.ppermute(over_x, axes, pairs(2, 3))], over_x


def gather_pieces(front, strip, child_map):
    owners = lax.axis_size(OWNER)
    rows, width = front.shape
    row_blocks = rows // BLK
    part = BLK // owners
    n_row = lax.axis_size("row")
    cut = front.reshape(row_blocks, owners // n_row, n_row, part, width)
    got = jnp.where(owner_of() == 0, cut[:, :, 0], 0.0)
    for r in range(1, n_row):
        got = got + lax.ppermute(cut[:, :, r], OWNER, [(0, r)])
    low = got[:, 0]
    high = lax.ppermute(got[:, 1], OWNER, [(r, n_row + r) for r in range(n_row)])
    panel, strips = pl.pallas_call(
        split_kernel,
        out_shape=[f32(owners, part, width), f32(owners, BLK, width)],
        in_specs=[SMEM, VMEM],
        out_specs=[VMEM] * 2,
        scratch_shapes=[pltpu.SMEM((child_map.shape[1],), jnp.int32)],
        compiler_params=PARAMS,
        name="split",
    )(child_map, strip)
    pieces = lax.all_to_all(panel, OWNER, split_axis=0, concat_axis=0, tiled=True)
    mine = pl.pallas_call(
        sum_panel_kernel,
        out_shape=f32(row_blocks, part, width),
        in_specs=[SMEM, VMEM, VMEM, VMEM],
        out_specs=VMEM,
        compiler_params=PARAMS,
        name="sum_panel",
    )(child_map, low, high, pieces)
    strips, mine = lax.optimization_barrier((strips, mine))
    others = [lax.ppermute(mine, "row", [(i, i ^ d) for i in range(n_row)]) for d in range(1, n_row)]
    near = jnp.stack([mine] + others)
    strips = lax.all_to_all(strips, OWNER, split_axis=0, concat_axis=0, tiled=True)
    far_top = lax.ppermute(near[:, : PIVOTS // BLK], "grp", [(0, 1), (1, 0)])
    return front, [near], [near, far_top], strips


def body(front, child_blocks, child_map):
    owners = lax.axis_size(OWNER)
    rows, width = front.shape
    blocks = owners * width // BLK
    few = lax.axis_size("grp") == 2 and lax.axis_size("row") == 4 and lax.axis_size("col") == 4
    few = few and BLK % (owners * 8) == 0 and child_map.shape[1] == blocks
    few = few and rows == 2 * width and width == PIVOTS
    gather = gather_pieces if few else gather_wide
    base, panel, pivot, last = gather(front, child_blocks[0], child_map)
    half = f32(BLK, BLK)
    cost = pl.CostEstimate(flops=8_000_000_000, bytes_accessed=1 << 18, transcendentals=0)
    upper, first, side, rest = pl.pallas_call(
        functools.partial(first_half_kernel, few),
        out_shape=[half] * 4,
        in_specs=[VMEM] * len(pivot),
        out_specs=[VMEM] * 4,
        scratch_shapes=[pltpu.VMEM((PIVOTS, PIVOTS), jnp.float32)],
        compiler_params=PARAMS,
        cost_estimate=cost,
        name="pivot_first",
    )(*pivot)
    if few:
        tops = PIVOTS // BLK
        near, far_top = pivot
        first, later = lax.optimization_barrier((first, near[:, tops:]))
        far_rest = lax.ppermute(later, "grp", [(0, 1), (1, 0)])
        panel = [near, far_top, far_rest]
        at = owner_of() * width % rows // BLK
        cut_near = lax.dynamic_slice_in_dim(near, at, width // BLK, 1)
        cut_far = jnp.where(at == 0, far_top, far_rest)
        own_part = jnp.concatenate([cut_near, cut_far], axis=0)
        parts, _ = over_col(own_part, [o * width // rows for o in range(owners)])
    upper2, inverse = pl.pallas_call(
        functools.partial(second_half_kernel, few),
        out_shape=[half, f32(PIVOTS, PIVOTS)],
        in_specs=[VMEM] * 3,
        out_specs=[VMEM] * 2,
        scratch_shapes=[pltpu.VMEM((BLK, BLK), jnp.float32)],
        compiler_params=PARAMS,
        cost_estimate=cost,
        name="pivot_second",
    )(first, side, rest)
    if few:
        inverses, _ = over_col(inverse, [0] * owners)
    else:
        inverses, parts = [inverse], [last]
    updated = pl.pallas_call(
        functools.partial(finish_kernel, few),
        out_shape=f32(rows, width),
        in_specs=[VMEM] * (4 + len(panel) + len(inverses) + len(parts)),
        out_specs=VMEM,
        scratch_shapes=[pltpu.VMEM((n, width), jnp.float32) for n in (rows, width, PIVOTS)],
        compiler_params=PARAMS,
        cost_estimate=pl.CostEstimate(flops=3_000_000_000, bytes_accessed=1 << 20, transcendentals=0),
        name="finish",
    )(base, *panel, upper, side, upper2, *inverses, *parts)
    if not few:
        return updated
    return pl.pallas_call(
        assemble_kernel,
        out_shape=f32(rows, width),
        in_specs=[SMEM, VMEM, VMEM],
        out_specs=VMEM,
        compiler_params=PARAMS,
        name="assemble",
    )(child_map, updated, last)


def solution(mesh):
    return jax.shard_map(
        body,
        mesh=mesh,
        in_specs=(P("col", ("grp", "row")), P("grp", ("row", "col"), None), P()),
        out_specs=P("col", ("grp", "row")),
        check_vma=False,
    )
```

```python
import functools

import jax
import jax.numpy as jnp
from jax import lax
from jax.experimental import pallas as pl
from jax.experimental.pallas import tpu as pltpu
from jax.sharding import PartitionSpec as P

BLK = 128
PIVOTS = 256
OWNER = ("grp", "row")
HIGHEST = lax.Precision.HIGHEST
SUB = 8
VMEM = pl.BlockSpec(memory_space=pltpu.VMEM)
SMEM = pl.BlockSpec(memory_space=pltpu.SMEM)
PARAMS = pltpu.CompilerParams(vmem_limit_bytes=48 * 1024 * 1024)


def f32(*shape):
    return jax.ShapeDtypeStruct(shape, jnp.float32)


def owner_of():
    return lax.axis_index("grp") * lax.axis_size("row") + lax.axis_index("row")


def dot(a, b, ca, cb):
    return lax.dot_general(
        a, b, (((ca,), (cb,)), ((), ())), precision=HIGHEST, preferred_element_type=jnp.float32
    )


def factor_small(cols):
    n = len(cols)
    d = [[cols[k][i] if i >= k else None for k in range(n)] for i in range(n)]
    low = [[None] * n for _ in range(n)]
    inv = [[None] * n for _ in range(n)]
    for k in range(n):
        root = lax.rsqrt(d[k][k])
        inv[k][k] = root
        for i in range(k + 1, n):
            low[i][k] = d[i][k] * root
        for i in range(k + 1, n):
            for j in range(k + 1, i + 1):
                d[i][j] = d[i][j] - low[i][k] * low[j][k]
        for j in range(k):
            total = low[k][j] * inv[j][j]
            for m in range(j + 1, k):
                total = total + low[k][m] * inv[m][j]
            inv[k][j] = -root * total
    return inv


def factor_block(groups):
    count = len(groups)
    shape = (SUB, BLK)
    sub = lax.broadcasted_iota(jnp.int32, shape, 0)
    lane = lax.broadcasted_iota(jnp.int32, shape, 1)
    spread_row = lambda v, i: jnp.broadcast_to(v[i : i + 1, :], shape)
    spread_col = lambda v, c: jnp.broadcast_to(v[:, c : c + 1], shape)
    upper, inverse = [], []
    groups = list(groups)
    for b in range(count):
        base = SUB * b
        cur = groups[b]
        here = [spread_col(cur, base + k) for k in range(SUB)]
        inv = factor_small([[spread_row(here[k], i) for i in range(SUB)] for k in range(SUB)])
        inv_col = []
        for k in range(SUB):
            col = jnp.where(sub == k, inv[k][k], 0.0)
            for i in range(k + 1, SUB):
                col = jnp.where(sub == i, inv[i][k], col)
            inv_col.append(col)
        done = inv_col[0] * spread_row(cur, 0)
        for k in range(1, SUB):
            done = done + inv_col[k] * spread_row(cur, k)
        upper.append(jnp.where(lane >= base + sub, done, 0.0))
        kept = done
        for k in range(SUB):
            kept = jnp.where(lane == base + k, inv_col[k], kept)
        inverse.append(jnp.where(lane <= base + sub, kept, 0.0))
        if b + 1 == count:
            break
        inside = (lane >= base) & (lane < base + SUB)
        for j in range(b + 1, min(b + 3, count)):
            nxt = groups[j]
            after = [spread_col(nxt, base + k) for k in range(SUB)]
            nxt = jnp.where(inside, 0.0, nxt)
            for i in range(SUB):
                low = after[0] * inv[i][0]
                for k in range(1, i + 1):
                    low = low + after[k] * inv[i][k]
                nxt = nxt - low * spread_row(kept, i)
            groups[j] = nxt
        if b + 3 < count:
            change = dot(done, kept, 0, 0)
            for j in range(b + 3, count):
                groups[j] = jnp.where(inside, 0.0, groups[j]) - change[SUB * j : SUB * (j + 1)]
    return upper, inverse


def factor_half(source, upper_ref, inverse_ref):
    upper, inverse = factor_block([source[SUB * g : SUB * (g + 1)] for g in range(BLK // SUB)])
    for g in range(BLK // SUB):
        at = slice(SUB * g, SUB * (g + 1))
        upper_ref[at, :] = upper[g]
        inverse_ref[at, :] = inverse[g]


def on_root(few):
    return lax.axis_index("col") == 0 if few else lax.axis_index("col") >= 0


def first_half_kernel(few, *refs):
    sources, (upper_ref, inverse_ref, side_ref, next_ref, pivot_ref) = refs[:-5], refs[-5:]

    @pl.when(on_root(few))
    def _():
        if few:
            grp = lax.axis_index("grp")
            tops = PIVOTS // BLK
            place_rows(pivot_ref, sources[0].at[:, :tops], grp)
            place_rows(pivot_ref, sources[1], 1 - grp)
        else:
            pivot_ref[...] = sources[0][...]
        factor_half(pivot_ref[:BLK, :BLK], upper_ref, inverse_ref)
        side = dot(inverse_ref[...], pivot_ref[:BLK, BLK:], 1, 0)
        side_ref[...] = side
        next_ref[...] = pivot_ref[BLK:, BLK:] - dot(side, side, 0, 0)


def second_half_kernel(few, first_ref, side_ref, next_ref, upper_ref, inverse_ref, second_ref):
    @pl.when(on_root(few))
    def _():
        factor_half(next_ref[...], upper_ref, second_ref)
        first, second = first_ref[...], second_ref[...]
        inverse_ref[:BLK, :BLK] = first
        inverse_ref[:BLK, BLK:] = jnp.zeros((BLK, BLK), jnp.float32)
        inverse_ref[BLK:, BLK:] = second
        inverse_ref[BLK:, :BLK] = -dot(second, dot(side_ref[...], first, 0, 0), 1, 0)


def split_kernel(map_ref, strip_ref, panel_ref, out_ref, inv_ref):
    owners, part, width = panel_ref.shape
    per = width // BLK
    grp = lax.axis_index("grp")
    for q in range(map_ref.shape[1]):
        inv_ref[map_ref[grp, q]] = q
    for k in range(owners):
        for s in range(per):
            at = pl.multiple_of(inv_ref[k * per + s] * BLK, BLK)
            out_ref[k, :, s * BLK : (s + 1) * BLK] = strip_ref[:, pl.ds(at, BLK)]
    for k in range(owners):
        panel_ref[k] = out_ref[0, part * k : part * (k + 1), :]


def sum_panel_kernel(map_ref, low_ref, high_ref, pieces_ref, out_ref):
    n_row, n_col = lax.axis_size("row"), lax.axis_size("col")
    grp, col = lax.axis_index("grp"), lax.axis_index("col")
    blocks = out_ref.shape[0]
    out_ref[...] = jnp.where(grp == 0, low_ref[...], high_ref[...])
    for i in range(pieces_ref.shape[0]):
        local = map_ref[i // n_row, i % n_row * n_col + col] - col * blocks
        out_ref[local] = out_ref[local] + pieces_ref[i]


def place_rows(target_ref, pieces_ref, grp, first=0):
    row = lax.axis_index("row")
    n_row, blocks, part, _ = pieces_ref.shape
    for b in range(blocks):
        for r in range(n_row):
            at = pl.multiple_of((first + b) * BLK + (grp * n_row + (row ^ r)) * part, SUB)
            target_ref[pl.ds(at, part), :] = pieces_ref[r, b]


def choose(refs, distance, take):
    for e, ref in enumerate(refs):
        pl.when(distance == e)(functools.partial(take, ref))


def assemble_kernel(map_ref, updated_ref, strips_ref, out_ref):
    n_row, n_col = lax.axis_size("row"), lax.axis_size("col")
    col = lax.axis_index("col")
    row_blocks = out_ref.shape[0] // BLK
    out_ref[...] = updated_ref[...]

    @pl.when(owner_of() != 0)
    def _():
        for i in range(strips_ref.shape[0]):
            local = map_ref[i // n_row, i % n_row * n_col + col] - col * row_blocks
            start = pl.multiple_of(local * BLK, BLK)
            out_ref[pl.ds(start, BLK), :] += strips_ref[i]

        @pl.when(col == 0)
        def _():
            out_ref[:PIVOTS, :] = jnp.zeros((PIVOTS, out_ref.shape[1]), jnp.float32)


def finish_kernel(few, base_ref, *refs):
    count = 3 if few else 1
    panel, (upper_ref, side_ref, upper2_ref), refs = refs[:count], refs[count : count + 3], refs[count + 3 :]
    count = lax.axis_size("col") if few else 1
    inverses, parts = refs[:count], refs[count : 2 * count]
    out_ref, rows_c_ref, rows_o_ref, inv_ref = refs[-4:]
    rows, width = out_ref.shape
    grp, col = lax.axis_index("grp"), lax.axis_index("col")
    me = owner_of()

    def take_inverse(ref):
        inv_ref[...] = ref[...]

    def take_part(ref):
        half = ref.shape[0] // 2
        place_rows(rows_o_ref, ref.at[:half], grp)
        place_rows(rows_o_ref, ref.at[half:], 1 - grp)

    if few:
        choose(inverses, col, take_inverse)
        choose(parts, (me * width // rows) ^ col, take_part)
        near_ref, far_top_ref, far_rest_ref = panel
        place_rows(rows_c_ref, near_ref, grp)
        place_rows(rows_c_ref, far_top_ref, 1 - grp)
        place_rows(rows_c_ref, far_rest_ref, 1 - grp, far_top_ref.shape[1])
    else:
        inv_ref[...] = inverses[0][...]
        rows_o_ref[...] = parts[0][...]
        rows_c_ref[...] = panel[0][...]
    inv = inv_ref[...]
    left = dot(rows_c_ref[...], inv, 1, 1)

    @pl.when(me == 0)
    def _():
        out_ref[...] = left

        @pl.when(col == 0)
        def _():
            out_ref[:BLK, :BLK] = upper_ref[...].T
            out_ref[:BLK, BLK:] = jnp.zeros((BLK, BLK), jnp.float32)
            out_ref[BLK:PIVOTS, :BLK] = side_ref[...].T
            out_ref[BLK:PIVOTS, BLK:] = upper2_ref[...].T

    @pl.when(me != 0)
    def _():
        right = dot(rows_o_ref[...], inv, 1, 1)
        out_ref[...] = base_ref[...] - dot(left, right, 1, 1)

        @pl.when(col == 0)
        def _():
            out_ref[:PIVOTS, :] = jnp.zeros((PIVOTS, width), jnp.float32)


def from_root(value, axis, root):
    mine = lax.axis_index(axis) == root
    return lax.psum(jnp.where(mine, value, jnp.zeros_like(value)), axis)


def gather_wide(front, strip, child_map):
    n_row, n_col = lax.axis_size("row"), lax.axis_size("col")
    owners = lax.axis_size(OWNER)
    rows, width = front.shape
    row_blocks = rows // BLK
    blocks = owners * width // BLK
    me = owner_of()
    col = lax.axis_index("col")
    hits = child_map[lax.axis_index("grp")][None, :] == jnp.arange(blocks)[:, None]
    source = jnp.argmax(hits, axis=1)
    taken = jnp.take(strip.reshape(BLK, -1, BLK), source, axis=1)
    taken = jnp.where(jnp.any(hits, axis=1)[None, :, None], taken, 0.0)
    outgoing = taken.reshape(BLK, owners, width).transpose(1, 0, 2)
    incoming = lax.all_to_all(outgoing, OWNER, split_axis=0, concat_axis=0, tiled=True)
    ids = jnp.arange(owners)
    places = child_map[ids // n_row, ids % n_row * n_col + col] - col * row_blocks
    assembled = front.reshape(row_blocks, BLK, width).at[places].add(incoming).reshape(rows, width)
    rows_c = from_root(assembled, OWNER, 0)
    pivot = from_root(rows_c[:PIVOTS], "col", 0)
    part = lax.dynamic_slice_in_dim(rows_c, me * width % rows, width, 0)
    rows_o = jnp.zeros((width, width), jnp.float32)
    for c in range(n_col):
        low = c * rows // width
        sent = from_root(part, "col", c)
        rows_o = jnp.where((me >= low) & (me < low + rows // width), sent, rows_o)
    return assembled, [rows_c], [pivot], rows_o


def over_col(value, roots):
    n_col = lax.axis_size("col")
    axes = OWNER + ("col",)
    pairs = lambda e, f: [(o * n_col + (c ^ e), o * n_col + (c ^ f)) for o, c in enumerate(roots)]
    over_x = lax.ppermute(value, axes, pairs(0, 2))
    beside = lax.ppermute(value, axes, pairs(0, 1))
    return [value, beside, over_x, lax.ppermute(over_x, axes, pairs(2, 3))], over_x


def gather_pieces(front, strip, child_map):
    owners = lax.axis_size(OWNER)
    rows, width = front.shape
    row_blocks = rows // BLK
    part = BLK // owners
    n_row = lax.axis_size("row")
    cut = front.reshape(row_blocks, owners // n_row, n_row, part, width)
    got = jnp.where(owner_of() == 0, cut[:, :, 0], 0.0)
    for r in range(1, n_row):
        got = got + lax.ppermute(cut[:, :, r], OWNER, [(0, r)])
    low = got[:, 0]
    high = lax.ppermute(got[:, 1], OWNER, [(r, n_row + r) for r in range(n_row)])
    panel, strips = pl.pallas_call(
        split_kernel,
        out_shape=[f32(owners, part, width), f32(owners, BLK, width)],
        in_specs=[SMEM, VMEM],
        out_specs=[VMEM] * 2,
        scratch_shapes=[pltpu.SMEM((child_map.shape[1],), jnp.int32)],
        compiler_params=PARAMS,
        name="split",
    )(child_map, strip)
    pieces = lax.all_to_all(panel, OWNER, split_axis=0, concat_axis=0, tiled=True)
    mine = pl.pallas_call(
        sum_panel_kernel,
        out_shape=f32(row_blocks, part, width),
        in_specs=[SMEM, VMEM, VMEM, VMEM],
        out_specs=VMEM,
        compiler_params=PARAMS,
        name="sum_panel",
    )(child_map, low, high, pieces)
    strips, mine = lax.optimization_barrier((strips, mine))
    others = [lax.ppermute(mine, "row", [(i, i ^ d) for i in range(n_row)]) for d in range(1, n_row)]
    near = jnp.stack([mine] + others)
    strips = lax.all_to_all(strips, OWNER, split_axis=0, concat_axis=0, tiled=True)
    far_top = lax.ppermute(near[:, : PIVOTS // BLK], "grp", [(0, 1), (1, 0)])
    return front, [near], [near, far_top], strips


def body(front, child_blocks, child_map):
    owners = lax.axis_size(OWNER)
    rows, width = front.shape
    blocks = owners * width // BLK
    few = lax.axis_size("grp") == 2 and lax.axis_size("row") == 4 and lax.axis_size("col") == 4
    few = few and BLK % (owners * 8) == 0 and child_map.shape[1] == blocks
    few = few and rows == 2 * width and width == PIVOTS
    gather = gather_pieces if few else gather_wide
    base, panel, pivot, last = gather(front, child_blocks[0], child_map)
    half = f32(BLK, BLK)
    cost = pl.CostEstimate(flops=500_000_000, bytes_accessed=1 << 18, transcendentals=0)
    upper, first, side, rest = pl.pallas_call(
        functools.partial(first_half_kernel, few),
        out_shape=[half] * 4,
        in_specs=[VMEM] * len(pivot),
        out_specs=[VMEM] * 4,
        scratch_shapes=[pltpu.VMEM((PIVOTS, PIVOTS), jnp.float32)],
        compiler_params=PARAMS,
        cost_estimate=cost,
        name="pivot_first",
    )(*pivot)
    if few:
        tops = PIVOTS // BLK
        near, far_top = pivot
        first, later = lax.optimization_barrier((first, near[:, tops:]))
        far_rest = lax.ppermute(later, "grp", [(0, 1), (1, 0)])
        panel = [near, far_top, far_rest]
        at = owner_of() * width % rows // BLK
        cut_near = lax.dynamic_slice_in_dim(near, at, width // BLK, 1)
        cut_far = jnp.where(at == 0, far_top, far_rest)
        own_part = jnp.concatenate([cut_near, cut_far], axis=0)
        parts, _ = over_col(own_part, [o * width // rows for o in range(owners)])
    upper2, inverse = pl.pallas_call(
        functools.partial(second_half_kernel, few),
        out_shape=[half, f32(PIVOTS, PIVOTS)],
        in_specs=[VMEM] * 3,
        out_specs=[VMEM] * 2,
        scratch_shapes=[pltpu.VMEM((BLK, BLK), jnp.float32)],
        compiler_params=PARAMS,
        cost_estimate=cost,
        name="pivot_second",
    )(first, side, rest)
    if few:
        inverses, _ = over_col(inverse, [0] * owners)
    else:
        inverses, parts = [inverse], [last]
    updated = pl.pallas_call(
        functools.partial(finish_kernel, few),
        out_shape=f32(rows, width),
        in_specs=[VMEM] * (4 + len(panel) + len(inverses) + len(parts)),
        out_specs=VMEM,
        scratch_shapes=[pltpu.VMEM((n, width), jnp.float32) for n in (rows, width, PIVOTS)],
        compiler_params=PARAMS,
        cost_estimate=pl.CostEstimate(flops=500_000_000, bytes_accessed=1 << 20, transcendentals=0),
        name="finish",
    )(base, *panel, upper, side, upper2, *inverses, *parts)
    if not few:
        return updated
    return pl.pallas_call(
        assemble_kernel,
        out_shape=f32(rows, width),
        in_specs=[SMEM, VMEM, VMEM],
        out_specs=VMEM,
        compiler_params=PARAMS,
        name="assemble",
    )(child_map, updated, last)


def solution(mesh):
    return jax.shard_map(
        body,
        mesh=mesh,
        in_specs=(P("col", ("grp", "row")), P("grp", ("row", "col"), None), P()),
        out_specs=P("col", ("grp", "row")),
        check_vma=False,
    )
```
